128 devices in a mesh: gy: 16 (over y_hi, x, core), gx: 8 (over y_lo, z).
Axes of the slice: x: 4, y: 4 (y_hi: 2, y_lo: 2; y = y_hi * 2 + y_lo), z: 4, core: 2. Of those that a mesh axis runs over, the one named last changes fastest.
Arguments:
- latent: bfloat16 [1, 4, 384, 128, 128], P(None, None, 'gy', 'gx'), may hold values from -6 to 6
- conv_one: bfloat16 [3, 3, 3, 128, 128], replicated, may hold values from -0.109375 to 0.109375
- conv_two: bfloat16 [3, 3, 3, 128, 128], replicated, may hold values from -0.109375 to 0.109375
- to_rgb: bfloat16 [3, 3, 3, 128, 3], replicated, may hold values from -0.1875 to 0.1875
- disc_one: bfloat16 [3, 3, 3, 3, 64], replicated, may hold values from -0.625 to 0.625
- disc_two: bfloat16 [3, 3, 3, 64, 128], replicated, may hold values from -0.15625 to 0.15625
- disc_head: float32 [128], replicated, may hold values from -4 to 4
Outputs:
- grad_latent: bfloat16 [1, 4, 384, 128, 128], P(None, None, 'gy', 'gx')
- logits: bfloat16 [1, 4, 384, 128], P(None, None, 'gy', 'gx')
The draws below stay inside these ranges and needn't reach their ends.
All inputs are finite; a program needn't handle non-finite values.
Results may differ from the reference program's by a relative error of at most 0.024.
Values may be sent and summed in bfloat16 or wider, within the bound.
No kernel may reach another device: no remote copies, remote signals or barrier semaphores. Data moves between devices by JAX's collectives and lax.ppermute only.
A program may use at most 64 MiB of HBM per device.

```python
import jax
import jax.numpy as jnp
from jax import lax

C = 128
C1 = 64
C2 = 128
FRAMES = 4
BATCH = 1
H = 384
W = 128


def block_scale(rng, shape, cuts, low, high):
    factor_of = 1.0
    for dim, blocks in cuts:
        draws = jax.random.uniform(jax.random.fold_in(jax.random.fold_in(rng, 6), dim), (blocks,), jnp.float32, low / len(cuts), high / len(cuts))
        factor_of = factor_of * jnp.repeat(jnp.exp(draws), shape[dim] // blocks).reshape((-1,) + (1,) * (len(shape) - 1 - dim))
    return factor_of


def normal_values(key, dims, scale, limit, shards=(), dtype=jnp.bfloat16):
    entries = scale * jax.random.normal(key, dims, jnp.float32)
    if shards:
        entries = entries * block_scale(key, dims, shards, -0.22, 0.18)
    return jnp.clip(entries, -limit, limit).astype(dtype)


def setup_inputs(seed: int = 0) -> dict:
    arg_keys = jax.random.split(jax.random.key(seed), 8)
    return {
        "latent": normal_values(arg_keys[0], (BATCH, FRAMES, H, W, C), 1.0, 6.0, ((2, 16), (3, 8))),
        "conv_one": normal_values(arg_keys[1], (3, 3, 3, C, C), (27 * C) ** -0.5, 0.109375),
        "conv_two": normal_values(arg_keys[2], (3, 3, 3, C, C), (27 * C) ** -0.5, 0.109375),
        "to_rgb": normal_values(arg_keys[3], (3, 3, 3, C, 3), (9 * C) ** -0.5, 0.1875),
        "disc_one": normal_values(arg_keys[4], (3, 3, 3, 3, C1), 81 ** -0.5, 0.625),
        "disc_two": normal_values(arg_keys[5], (3, 3, 3, C1, C2), (27 * C1) ** -0.5, 0.15625),
        "disc_head": normal_values(arg_keys[6], (C2,), 1.0, 4.0, (), jnp.float32),
    }


LAST_FORM = "btyxc,cd->btyxd"
TO_FIRST = "btyxc,cd->btdyx"
TO_LAST = "btcyx,cd->btyxd"


def convolve(widened, kernel, form, row_dim, forward):
    if forward:
        frame_pad = (2, 0)
        taps = kernel
    else:
        frame_pad = (0, 2)
        taps = jnp.swapaxes(jnp.flip(kernel, (0, 1, 2)), 3, 4)
    widths = [(0, 0)] * widened.ndim
    widths[1] = frame_pad
    padded = jnp.pad(widened, widths)
    frames = widened.shape[1]
    rows = widened.shape[row_dim] - 2
    cols = widened.shape[row_dim + 1] - 2
    total = None
    for depth in range(3):
        for row_tap in range(3):
            for col_tap in range(3):
                piece = lax.slice_in_dim(padded, depth, depth + frames, axis=1)
                piece = lax.slice_in_dim(piece, row_tap, row_tap + rows, axis=row_dim)
                piece = lax.slice_in_dim(piece, col_tap, col_tap + cols, axis=row_dim + 1)
                term = jnp.einsum(form, piece.astype(jnp.float32), taps[depth, row_tap, col_tap].astype(jnp.float32))
                total = term if total is None else total + term
    return total


def spread(field, row_dim):
    widths = [(0, 0)] * field.ndim
    widths[row_dim] = (1, 1)
    widths[row_dim + 1] = (1, 1)
    return jnp.pad(field, widths)


def dsilu(value):
    sigma = jax.nn.sigmoid(value)
    return sigma * (1.0 + value * (1.0 - sigma))


def reference(latent, conv_one, conv_two, to_rgb, disc_one, disc_two, disc_head):
    pre_one = convolve(spread(latent, 2), conv_one, LAST_FORM, 2, True)
    act_one = jax.nn.silu(pre_one).astype(jnp.bfloat16)
    pre_two = convolve(spread(act_one, 2), conv_two, LAST_FORM, 2, True)
    act_two = jax.nn.silu(pre_two).astype(jnp.bfloat16)
    rgb = convolve(spread(act_two, 2), to_rgb, TO_FIRST, 2, True).astype(jnp.bfloat16)
    pre_first = convolve(spread(rgb, 3), disc_one, TO_LAST, 3, True)
    act_first = jax.nn.silu(pre_first).astype(jnp.bfloat16)
    pre_second = convolve(spread(act_first, 2), disc_two, LAST_FORM, 2, True)
    scores = jnp.einsum("btyxd,d->btyx", jax.nn.silu(pre_second), disc_head, precision=lax.Precision.HIGHEST)
    push = -jax.nn.sigmoid(-scores)
    back_second = (push[..., None] * disc_head * dsilu(pre_second)).astype(jnp.bfloat16)
    back_act = convolve(spread(back_second, 2), disc_two, LAST_FORM, 2, False)
    back_first = (back_act * dsilu(pre_first)).astype(jnp.bfloat16)
    pixel_grad = convolve(spread(back_first, 2), disc_one, TO_FIRST, 2, False).astype(jnp.bfloat16)
    back_rgb = convolve(spread(pixel_grad, 3), to_rgb, TO_LAST, 3, False)
    back_two = (back_rgb * dsilu(pre_two)).astype(jnp.bfloat16)
    back_mid = convolve(spread(back_two, 2), conv_two, LAST_FORM, 2, False)
    back_one = (back_mid * dsilu(pre_one)).astype(jnp.bfloat16)
    grad_latent = convolve(spread(back_one, 2), conv_one, LAST_FORM, 2, False).astype(jnp.bfloat16)
    return grad_latent, scores.astype(jnp.bfloat16)
```

```python
import jax
import jax.numpy as jnp
import numpy as np
from jax import lax
from jax.experimental import pallas as pl
from jax.experimental.pallas import tpu as pltpu
from jax.sharding import PartitionSpec as P

F32 = jnp.float32
BF16 = jnp.bfloat16

HALO = 10
ROWS, COLS = 24, 16
TALL = 48
SHORT = 32
WIDE = COLS + 2 * HALO
HIGH = ROWS + 2 * HALO
PAD = 64


def width(h):
    return COLS + 2 * h


def sigmoid(v):
    return 0.5 * jnp.tanh(0.5 * v) + 0.5


def silu(v):
    return v * sigmoid(v)


def dsilu(v):
    s = sigmoid(v)
    return s * (1.0 + v * (1.0 - s))


def pair_weights(k):
    k = jnp.transpose(k, (0, 2, 1, 3, 4))
    zero = jnp.zeros_like(k[0])
    far = jnp.stack([jnp.stack([k[0], zero], 3), jnp.stack([k[1], k[0]], 3)], 2)
    near = jnp.stack([jnp.stack([k[2], k[1]], 3), jnp.stack([zero, k[2]], 3)], 2)
    ci, co = k.shape[-2:]
    return jnp.concatenate([far.reshape(9 * 2 * ci, 2 * co), near.reshape(9 * 2 * ci, 2 * co)], 0)


def pair_weights_back(k):
    k = jnp.transpose(jnp.flip(k, (1, 2)), (0, 2, 1, 4, 3))
    zero = jnp.zeros_like(k[0])
    far = jnp.stack([jnp.stack([k[0], k[1]], 3), jnp.stack([zero, k[0]], 3)], 2)
    near = jnp.stack([jnp.stack([k[2], zero], 3), jnp.stack([k[1], k[2]], 3)], 2)
    ci, co = k.shape[-2:]
    return jnp.concatenate([far.reshape(9 * 2 * ci, 2 * co), near.reshape(9 * 2 * ci, 2 * co)], 0)


def frame_blocks(k, back):
    zero = jnp.zeros_like(k[0])

    def tap(i, o):
        d = o - i if not back else i - o
        return k[2 - d] if 0 <= d <= 2 else zero

    return jnp.stack([jnp.stack([tap(i, o) for o in range(4)]) for i in range(4)])


def fold_last(k, back):
    if back:
        k = jnp.swapaxes(jnp.flip(k, (1, 2)), 3, 4)
    b = frame_blocks(jnp.swapaxes(k, 1, 2), back)
    b = jnp.transpose(b, (0, 4, 2, 3, 1, 5))
    b = b.reshape(b.shape[0] * b.shape[1], -1)
    return jnp.pad(b, ((0, 0), (0, 128 - b.shape[1])))


def fold_first(k, back):
    if back:
        k = jnp.swapaxes(jnp.flip(k, (1, 2)), 3, 4)
    b = frame_blocks(jnp.swapaxes(k, 1, 2), back)
    b = jnp.transpose(b, (2, 3, 0, 4, 1, 5))
    b = b.reshape(-1, b.shape[-2] * b.shape[-1])
    return jnp.pad(b, ((0, 128 - b.shape[0]), (0, 0)))


def second_weights(k):
    b = frame_blocks(jnp.swapaxes(k, 1, 2), False)
    b = jnp.transpose(b, (2, 3, 0, 4, 1, 5))
    low = b[:, :, :2, :, :2].reshape(9 * 128, 256)
    high = b[:, :, :, :, 2:].reshape(9 * 256, 256)
    return jnp.concatenate([low, high], 0)


def second_weights_back(k):
    k = jnp.swapaxes(jnp.flip(k, (1, 2)), 3, 4)
    b = frame_blocks(jnp.swapaxes(k, 1, 2), True)
    b = jnp.transpose(b, (2, 3, 0, 4, 1, 5))
    return b.reshape(9 * 512, 256)


def kernel(
    x_ref, w1_hbm, w2_hbm, rgb_w, one_w, sec_hbm, head, secb_hbm, oneb_w, rgbb_w, w2b_hbm, w1b_hbm,
    out_ref, logit_ref,
    field, pre1, pre2, pref, taps, valid, valid_s, part, pix, w1, w2, sec, secb, w2b, w1b, sems,
):
    loads = [
        pltpu.make_async_copy(a, b, sems.at[n])
        for n, (a, b) in enumerate(
            [(w1_hbm, w1), (w2_hbm, w2), (sec_hbm, sec), (secb_hbm, secb), (w2b_hbm, w2b), (w1b_hbm, w1b)]
        )
    ]
    for c in loads:
        c.start()
    gy, gx = lax.axis_index("gy"), lax.axis_index("gx")
    ny, nx = lax.axis_size("gy"), lax.axis_size("gx")

    def validity(ref, stride, h):
        first_x, first_y = gx * COLS - h, gy * ROWS - h
        y = first_y + lax.broadcasted_iota(jnp.int32, (stride, 128), 0)
        good_y = jnp.where((y >= 0) & (y < ny * ROWS), 1.0, 0.0).astype(F32)

        def body(x, _):
            place = first_x + x
            good_x = jnp.where((place >= 0) & (place < nx * COLS), 1.0, 0.0).astype(F32)
            ref[pl.ds(pl.multiple_of(x * stride, 8), stride), :] = good_y * good_x
            return 0

        lax.fori_loop(0, width(h), body, 0)

    validity(valid, TALL, HALO)
    validity(valid_s, SHORT, 2)

    def spread(count, stride, tiles, mask=None):
        step = 96

        def body(n, _):
            r = pl.multiple_of(n * step, 32)
            for j in range(3):
                good = None if mask is None else mask[pl.ds(r + j, step), :] > 0
                for t in range(tiles):
                    v = field[t, pl.ds(r + j, step), :]
                    if good is not None:
                        v = jnp.where(good, v, 0.0)
                    taps[j, pl.ds(r, step), t * 128 : t * 128 + 128] = v.astype(BF16)
            return 0

        lax.fori_loop(0, -(-count * stride // step), body, 0)

    def operand(base, rows, stride, tiles):
        return jnp.concatenate(
            [
                taps[j, pl.ds(pl.multiple_of(base + l * stride, 16), rows), tiles[0] * 128 : tiles[1] * 128]
                for l in range(3)
                for j in range(3)
            ],
            1,
        )

    def dot(a, b):
        return jnp.dot(a, b, preferred_element_type=F32)

    for t in range(4):
        def body(y, _, t=t):
            field[t, pl.ds(y, WIDE, TALL), :] = x_ref[t, y].astype(F32)
            return 0

        lax.fori_loop(0, HIGH, body, 0)
    spread(WIDE, TALL, 4, valid)

    def decode(w, pre, h, columns):
        rows = columns * TALL
        off = (HALO - h) * (TALL + 1)

        def body(n, _):
            base = pl.multiple_of(n * rows, 16)
            good = valid[pl.ds(base + off, rows), :] > 0
            near, far = operand(base, rows, TALL, (0, 2)), operand(base, rows, TALL, (2, 4))
            low = dot(near, w[2304:])
            high = dot(near, w[:2304]) + dot(far, w[2304:])
            for t, (v, s) in enumerate(((low, 0), (low, 128), (high, 0), (high, 128))):
                v = v[:, s : s + 128]
                pre[t, pl.ds(base, rows), :] = v
                field[t, pl.ds(base, rows), :] = jnp.where(good, silu(v), 0.0)
            return 0

        lax.fori_loop(0, width(h) // columns, body, 0)

    loads[0].wait()
    decode(w1, pre1, 9, 17)
    spread(width(9), TALL, 4)
    loads[1].wait()
    decode(w2, pre2, 8, 16)

    def gather_taps(count, h):
        off = (HALO - h) * (TALL + 1)
        lane = lax.broadcasted_iota(jnp.int32, (TALL, 128), 1)

        def rows(x, _):
            base = pl.multiple_of(x * TALL, 8)
            total = None
            for l in range(3):
                q = None
                for j in range(3):
                    v = part[pl.ds(base + l * TALL + j, TALL), :]
                    v = pltpu.roll(v, (128 - 12 * j) % 128, 1) if j else v
                    q = v if q is None else q + v
                q = pltpu.roll(q, (128 - 36 * l) % 128, 1) if l else q
                total = q if total is None else total + q
            good = (valid[pl.ds(base + off, TALL), :] > 0) & (lane < 12)
            pix[pl.ds(base, TALL), :] = jnp.where(good, total, 0.0).astype(BF16).astype(F32)
            return 0

        lax.fori_loop(0, count, rows, 0)

    def scatter_taps(count, stride):
        def rows(x, _):
            base = pl.multiple_of(x * TALL, 8)
            total = None
            for l in range(3):
                q = None
                for j in range(3):
                    v = pix[pl.ds(base + l * TALL + j, stride), :]
                    v = pltpu.roll(v, 12 * j, 1) if j else v
                    q = v if q is None else q + v
                q = pltpu.roll(q, 36 * l, 1) if l else q
                total = q if total is None else total + q
            taps[0, pl.ds(pl.multiple_of(x * stride, 16), stride), 0:128] = total.astype(BF16)
            return 0

        lax.fori_loop(0, count, rows, 0)

    def rgb_part(n, _):
        rows = 16 * TALL
        base = pl.multiple_of(n * rows, 16)
        a = jnp.concatenate([field[t, pl.ds(base, rows), :].astype(BF16) for t in range(4)], 1)
        part[pl.ds(base, rows), :] = dot(a, rgb_w[...])
        return 0

    lax.fori_loop(0, width(8) // 16, rgb_part, 0)
    gather_taps(width(7), 7)

    scatter_taps(width(6), TALL)

    def first(n, _):
        rows = 14 * TALL
        base = pl.multiple_of(n * rows, 16)
        good = valid[pl.ds(base + 4 * (TALL + 1), rows), :] > 0
        v = dot(taps[0, pl.ds(base, rows), 0:128], one_w[...])
        for t in range(2):
            p = v[:, t * 128 : t * 128 + 128]
            pref[t, pl.ds(base, rows), :] = p
            field[t, pl.ds(base, rows), :] = jnp.where(good, silu(p), 0.0)
        return 0

    lax.fori_loop(0, 2, first, 0)
    spread(width(6), TALL, 2)
    loads[2].wait()

    def second(n, _):
        rows = 13 * TALL
        base = pl.multiple_of(n * rows, 16)
        good = valid[pl.ds(base + 5 * (TALL + 1), rows), :] > 0
        low = dot(operand(base, rows, TALL, (0, 1)), sec[:1152])
        high = dot(operand(base, rows, TALL, (0, 2)), sec[1152:])
        lane = lax.broadcasted_iota(jnp.int32, (rows, 128), 1)
        logits = jnp.zeros((rows, 128), F32)
        for t, (v, s) in enumerate(((low, 0), (low, 128), (high, 0), (high, 128))):
            v = v[:, s : s + 128]
            sg = sigmoid(v)
            score = jnp.sum(v * sg * head[...], axis=1, keepdims=True)
            push = -sigmoid(-score)
            logits = jnp.where(lane == t, score, logits)
            g = push * head[...] * (sg * (1.0 + v * (1.0 - sg)))
            field[t, pl.ds(base, rows), :] = jnp.where(good, g, 0.0)
        part[pl.ds(base, rows), :] = logits
        return 0

    lax.fori_loop(0, 2, second, 0)
    for x in range(COLS):
        logit_ref[x] = part[pl.ds((x + 5) * TALL + 5, ROWS), :]
    spread(width(5), TALL, 4)
    loads[3].wait()

    def second_back(n, _):
        rows = 12 * TALL
        base = pl.multiple_of(n * rows, 16)
        good = valid[pl.ds(base + 6 * (TALL + 1), rows), :] > 0
        v = dot(operand(base, rows, TALL, (0, 4)), secb[...])
        g = []
        for t in range(2):
            p = pref[t, pl.ds(base + 2 * (TALL + 1), rows), :]
            g.append(jnp.where(good, v[:, t * 128 : t * 128 + 128] * dsilu(p), 0.0).astype(BF16))
        part[pl.ds(base, rows), :] = dot(jnp.concatenate(g, 1), oneb_w[...])
        return 0

    lax.fori_loop(0, 2, second_back, 0)
    gather_taps(width(3), 3)

    scatter_taps(width(2), SHORT)
    back = dot(taps[0, 0 : width(2) * SHORT, 0:128], rgbb_w[...])
    for t in range(4):
        for x in range(width(2)):
            p = pre2[t, pl.ds((x + 6) * TALL + 6, SHORT), :]
            g = back[x * SHORT : (x + 1) * SHORT, t * 128 : t * 128 + 128] * dsilu(p)
            good = valid_s[pl.ds(x * SHORT, SHORT), :] > 0
            field[t, pl.ds(x * SHORT, SHORT), :] = jnp.where(good, g, 0.0)
    spread(width(2), SHORT, 4)

    def back_conv(w, count):
        rows = count * SHORT
        near, far = operand(0, rows, SHORT, (0, 2)), operand(0, rows, SHORT, (2, 4))
        high = dot(far, w[2304:])
        low = dot(far, w[:2304]) + dot(near, w[2304:])
        return [v[:, s : s + 128] for v in (low, high) for s in (0, 128)]

    loads[4].wait()
    back = back_conv(w2b, width(1))
    for t in range(4):
        for x in range(width(1)):
            p = pre1[t, pl.ds((x + 8) * TALL + 8, SHORT), :]
            g = back[t][x * SHORT : (x + 1) * SHORT] * dsilu(p)
            good = valid_s[pl.ds((x + 1) * SHORT + 1, SHORT), :] > 0
            field[t, pl.ds(x * SHORT, SHORT), :] = jnp.where(good, g, 0.0)
    spread(width(1), SHORT, 4)
    loads[5].wait()
    back = back_conv(w1b, width(0))
    for t in range(4):
        field[t, 0 : COLS * SHORT, :] = back[t]
    for t in range(4):
        for y in range(ROWS):
            out_ref[t, y] = field[t, pl.ds(y, COLS, SHORT), :].astype(BF16)


def per_device(latent, conv_one, conv_two, to_rgb, disc_one, disc_two, disc_head):
    x = latent[0]

    def widen(v, axis, dim):
        n = lax.axis_size(axis)
        size = v.shape[dim]
        before = lax.ppermute(
            lax.slice_in_dim(v, size - HALO, size, axis=dim), axis, [(i, (i + 1) % n) for i in range(n)]
        )
        after = lax.ppermute(
            lax.slice_in_dim(v, 0, HALO, axis=dim), axis, [((i + 1) % n, i) for i in range(n)]
        )
        return jnp.concatenate([before, v, after], dim)

    x = widen(x, "gx", 2)
    x = widen(x, "gy", 1)
    weights = (
        pair_weights(conv_one),
        pair_weights(conv_two),
        fold_last(to_rgb, False),
        fold_first(disc_one, False),
        second_weights(disc_two),
        disc_head.reshape(1, 128),
        second_weights_back(disc_two),
        fold_last(disc_one, True),
        fold_first(to_rgb, True),
        pair_weights_back(conv_two),
        pair_weights_back(conv_one),
    )
    vmem = pl.BlockSpec(memory_space=pltpu.VMEM)
    hbm = pl.BlockSpec(memory_space=pl.ANY)
    p = WIDE * TALL + PAD
    out, logits = pl.pallas_call(
        kernel,
        out_shape=[
            jax.ShapeDtypeStruct((4, ROWS, COLS, 128), BF16),
            jax.ShapeDtypeStruct((COLS, ROWS, 128), F32),
        ],
        in_specs=[vmem, hbm, hbm, vmem, vmem, hbm, vmem, hbm, vmem, vmem, hbm, hbm],
        out_specs=[vmem, vmem],
        scratch_shapes=[
            pltpu.VMEM((4, p, 128), F32),
            pltpu.VMEM((4, p, 128), F32),
            pltpu.VMEM((4, p, 128), F32),
            pltpu.VMEM((2, p, 128), F32),
            pltpu.VMEM((3, p, 512), BF16),
            pltpu.VMEM((p, 128), F32),
            pltpu.VMEM((p, 128), F32),
            pltpu.VMEM((p, 128), F32),
            pltpu.VMEM((p, 128), F32),
        ]
        + [pltpu.VMEM(weights[n].shape, BF16) for n in (0, 1, 4, 6, 9, 10)]
        + [pltpu.SemaphoreType.DMA((6,))],
        compiler_params=pltpu.CompilerParams(vmem_limit_bytes=56 << 20),
    )(x, *weights)
    logits = jnp.transpose(logits[:, :, :4], (2, 1, 0)).astype(BF16)
    return out[None], logits[None]


def solution(mesh):
    placed = (P(None, None, "gy", "gx", None), P(), P(), P(), P(), P(), P())
    return jax.shard_map(
        per_device,
        mesh=mesh,
        in_specs=placed,
        out_specs=(P(None, None, "gy", "gx", None), P(None, None, "gy", "gx")),
        check_vma=False,
    )
```

```python
import jax
import jax.numpy as jnp
import numpy as np
from jax import lax
from jax.experimental import pallas as pl
from jax.experimental.pallas import tpu as pltpu
from jax.sharding import PartitionSpec as P

F32 = jnp.float32
BF16 = jnp.bfloat16

HALO = 10
ROWS, COLS = 24, 16
TALL = 48
SHORT = 32
WIDE = COLS + 2 * HALO
HIGH = ROWS + 2 * HALO
PAD = 64


def width(h):
    return COLS + 2 * h


def sigmoid(v):
    return 0.5 * jnp.tanh(0.5 * v) + 0.5


def silu(v):
    return v * sigmoid(v)


def dsilu(v):
    s = sigmoid(v)
    return s * (1.0 + v * (1.0 - s))


def kernel(
    x_ref, k1, k2, ks, rgb_rows, one_rows, head,
    out_ref, logit_ref,
    field, pre1, pre2, pref, taps, valid, valid_s, part, pix, w1, w2, sec, small, rgb_w, one_w, sems,
):
    loads = []
    for n, (k, w) in enumerate(((k1, w1), (k2, w2))):
        for far in range(2):
            for f in range(2):
                for t in range(2):
                    i = f - t + 2 - 2 * far
                    block = w.at[far, :, f * 128 : f * 128 + 128, t * 128 : t * 128 + 128]
                    if 0 <= i <= 2:
                        loads.append((n, pltpu.make_async_copy(k.at[i], block, sems.at[len(loads)])))
                    else:
                        block[...] = jnp.zeros(block.shape, BF16)
    for f in range(4):
        for t in range(4):
            i = f - t + 2
            block = sec.at[:, f * 64 : f * 64 + 64, t * 128 : t * 128 + 128]
            if 0 <= i <= 2:
                loads.append((2, pltpu.make_async_copy(ks.at[i], block, sems.at[len(loads)])))
            else:
                block[...] = jnp.zeros(block.shape, BF16)
    for _, c in loads:
        c.start()

    def arrived(which):
        for n, c in loads:
            if n == which:
                c.wait()

    small[...] = jnp.zeros_like(small)
    for rows, out, lanes in ((rgb_rows, rgb_w, 128), (one_rows, one_w, 64)):
        for f in range(4):
            for t in range(4):
                i = (t - f if out is rgb_w else f - t) + 2
                if 0 <= i <= 2:
                    for n in range(9):
                        small[n * 12 + f * 3 : n * 12 + f * 3 + 3, t * lanes : t * lanes + lanes] = rows[
                            (i * 9 + n) * 3 : (i * 9 + n) * 3 + 3, 0:lanes
                        ]
        out[...] = small[:, 0 : 4 * lanes].astype(BF16)
        if out is rgb_w:
            small[...] = jnp.zeros_like(small)

    gy, gx = lax.axis_index("gy"), lax.axis_index("gx")
    ny, nx = lax.axis_size("gy"), lax.axis_size("gx")

    def validity(ref, stride, h):
        first_x, first_y = gx * COLS - h, gy * ROWS - h
        y = first_y + lax.broadcasted_iota(jnp.int32, (stride, 128), 0)
        good_y = jnp.where((y >= 0) & (y < ny * ROWS), 1.0, 0.0).astype(F32)

        def body(x, _):
            place = first_x + x
            good_x = jnp.where((place >= 0) & (place < nx * COLS), 1.0, 0.0).astype(F32)
            ref[pl.ds(pl.multiple_of(x * stride, 8), stride), :] = good_y * good_x
            return 0

        lax.fori_loop(0, width(h), body, 0)

    validity(valid, TALL, HALO)
    validity(valid_s, SHORT, 2)

    def spread(count, stride, tiles, mask=None):
        step = 96

        def body(n, _):
            r = pl.multiple_of(n * step, 32)
            for j in range(3):
                good = None if mask is None else mask[pl.ds(r + j, step), :] > 0
                for t in range(tiles):
                    v = field[t, pl.ds(r + j, step), :]
                    if good is not None:
                        v = jnp.where(good, v, 0.0)
                    taps[j, pl.ds(r, step), t * 128 : t * 128 + 128] = v.astype(BF16)
            return 0

        lax.fori_loop(0, -(-count * stride // step), body, 0)

    def operand(base, rows, stride, tiles):
        return jnp.concatenate(
            [
                taps[j, pl.ds(pl.multiple_of(base + l * stride, 16), rows), tiles[0] * 128 : tiles[1] * 128]
                for j in range(3)
                for l in range(3)
            ],
            1,
        )

    def stack(w, rows=slice(None), lanes=slice(None)):
        v = w[:, rows, lanes]
        return v.reshape(-1, v.shape[-1])

    def across(w):
        return jnp.concatenate([w[8 - n] for n in range(9)], 1)

    def dot_t(a, b):
        return lax.dot_general(a, b, (((1,), (1,)), ((), ())), preferred_element_type=F32)

    def dot(a, b):
        return jnp.dot(a, b, preferred_element_type=F32)

    for t in range(4):
        def body(y, _, t=t):
            field[t, pl.ds(y, WIDE, TALL), :] = x_ref[t, y].astype(F32)
            return 0

        lax.fori_loop(0, HIGH, body, 0)
    spread(WIDE, TALL, 4, valid)

    def decode(w, pre, h, columns):
        rows = columns * TALL
        off = (HALO - h) * (TALL + 1)

        def body(n, _):
            base = pl.multiple_of(n * rows, 16)
            good = valid[pl.ds(base + off, rows), :] > 0
            near, far = operand(base, rows, TALL, (0, 2)), operand(base, rows, TALL, (2, 4))
            low = dot(near, stack(w.at[0]))
            high = dot(near, stack(w.at[1])) + dot(far, stack(w.at[0]))
            for t, (v, s) in enumerate(((low, 0), (low, 128), (high, 0), (high, 128))):
                v = v[:, s : s + 128]
                pre[t, pl.ds(base, rows), :] = v
                field[t, pl.ds(base, rows), :] = jnp.where(good, silu(v), 0.0)
            return 0

        lax.fori_loop(0, width(h) // columns, body, 0)

    arrived(0)
    decode(w1, pre1, 9, 17)
    spread(width(9), TALL, 4)
    arrived(1)
    decode(w2, pre2, 8, 16)

    def gather_taps(count, h, flip):
        off = (HALO - h) * (TALL + 1)
        lane = lax.broadcasted_iota(jnp.int32, (TALL, 128), 1)

        def rows(x, _):
            base = pl.multiple_of(x * TALL, 8)
            total = None
            for j in range(3):
                q = None
                for l in range(3):
                    v = part[pl.ds(base + l * TALL + j, TALL), :]
                    group = 2 - l if flip else l
                    v = pltpu.roll(v, 128 - 12 * group, 1) if group else v
                    q = v if q is None else q + v
                group = 2 - j if flip else j
                q = pltpu.roll(q, 128 - 36 * group, 1) if group else q
                total = q if total is None else total + q
            good = (valid[pl.ds(base + off, TALL), :] > 0) & (lane < 12)
            pix[pl.ds(base, TALL), :] = jnp.where(good, total, 0.0).astype(BF16).astype(F32)
            return 0

        lax.fori_loop(0, count, rows, 0)

    def scatter_taps(count, stride, flip):
        def rows(x, _):
            base = pl.multiple_of(x * TALL, 8)
            total = None
            for j in range(3):
                q = None
                for l in range(3):
                    v = pix[pl.ds(base + l * TALL + j, stride), :]
                    group = 2 - l if flip else l
                    v = pltpu.roll(v, 12 * group, 1) if group else v
                    q = v if q is None else q + v
                group = 2 - j if flip else j
                q = pltpu.roll(q, 36 * group, 1) if group else q
                total = q if total is None else total + q
            taps[0, pl.ds(pl.multiple_of(x * stride, 16), stride), 0:128] = total.astype(BF16)
            return 0

        lax.fori_loop(0, count, rows, 0)

    def rgb_part(n, _):
        rows = 16 * TALL
        base = pl.multiple_of(n * rows, 16)
        a = jnp.concatenate([field[t, pl.ds(base, rows), :].astype(BF16) for t in range(4)], 1)
        part[pl.ds(base, rows), :] = dot_t(a, rgb_w[...])
        return 0

    lax.fori_loop(0, width(8) // 16, rgb_part, 0)
    gather_taps(width(7), 7, False)

    scatter_taps(width(6), TALL, False)

    def first(n, _):
        rows = 14 * TALL
        base = pl.multiple_of(n * rows, 16)
        good = valid[pl.ds(base + 4 * (TALL + 1), rows), :] > 0
        v = dot(taps[0, pl.ds(base, rows), 0:128], one_w[...])
        for t in range(2):
            p = v[:, t * 128 : t * 128 + 128]
            pref[t, pl.ds(base, rows), :] = p
            field[t, pl.ds(base, rows), :] = jnp.where(good, silu(p), 0.0)
        return 0

    lax.fori_loop(0, 2, first, 0)
    spread(width(6), TALL, 2)
    arrived(2)

    def second(n, _):
        rows = 13 * TALL
        base = pl.multiple_of(n * rows, 16)
        good = valid[pl.ds(base + 5 * (TALL + 1), rows), :] > 0
        low = dot(operand(base, rows, TALL, (0, 1)), stack(sec, slice(0, 128), slice(0, 256)))
        high = dot(operand(base, rows, TALL, (0, 2)), stack(sec, slice(None), slice(256, 512)))
        lane = lax.broadcasted_iota(jnp.int32, (rows, 128), 1)
        logits = jnp.zeros((rows, 128), F32)
        for t, (v, s) in enumerate(((low, 0), (low, 128), (high, 0), (high, 128))):
            v = v[:, s : s + 128]
            sg = sigmoid(v)
            score = jnp.sum(v * sg * head[...], axis=1, keepdims=True)
            push = -sigmoid(-score)
            logits = jnp.where(lane == t, score, logits)
            g = push * head[...] * (sg * (1.0 + v * (1.0 - sg)))
            field[t, pl.ds(base, rows), :] = jnp.where(good, g, 0.0)
        part[pl.ds(base, rows), :] = logits
        return 0

    lax.fori_loop(0, 2, second, 0)
    for x in range(COLS):
        logit_ref[x] = part[pl.ds((x + 5) * TALL + 5, ROWS), :]
    spread(width(5), TALL, 4)

    def second_back(n, _):
        rows = 12 * TALL
        base = pl.multiple_of(n * rows, 16)
        good = valid[pl.ds(base + 6 * (TALL + 1), rows), :] > 0
        v = dot_t(operand(base, rows, TALL, (0, 4)), across(sec))
        g = []
        for t in range(2):
            p = pref[t, pl.ds(base + 2 * (TALL + 1), rows), :]
            g.append(jnp.where(good, v[:, t * 128 : t * 128 + 128] * dsilu(p), 0.0).astype(BF16))
        part[pl.ds(base, rows), :] = dot_t(jnp.concatenate(g, 1), one_w[...])
        return 0

    lax.fori_loop(0, 2, second_back, 0)
    gather_taps(width(3), 3, True)

    scatter_taps(width(2), SHORT, True)
    back = dot(taps[0, 0 : width(2) * SHORT, 0:128], rgb_w[...])
    for t in range(4):
        for x in range(width(2)):
            p = pre2[t, pl.ds((x + 6) * TALL + 6, SHORT), :]
            g = back[x * SHORT : (x + 1) * SHORT, t * 128 : t * 128 + 128] * dsilu(p)
            good = valid_s[pl.ds(x * SHORT, SHORT), :] > 0
            field[t, pl.ds(x * SHORT, SHORT), :] = jnp.where(good, g, 0.0)
    spread(width(2), SHORT, 4)

    def back_conv(w, count):
        rows = count * SHORT
        near, far = operand(0, rows, SHORT, (0, 2)), operand(0, rows, SHORT, (2, 4))
        high = dot_t(far, across(w.at[0]))
        low = dot_t(far, across(w.at[1])) + dot_t(near, across(w.at[0]))
        return [v[:, s : s + 128] for v in (low, high) for s in (0, 128)]

    back = back_conv(w2, width(1))
    for t in range(4):
        for x in range(width(1)):
            p = pre1[t, pl.ds((x + 8) * TALL + 8, SHORT), :]
            g = back[t][x * SHORT : (x + 1) * SHORT] * dsilu(p)
            good = valid_s[pl.ds((x + 1) * SHORT + 1, SHORT), :] > 0
            field[t, pl.ds(x * SHORT, SHORT), :] = jnp.where(good, g, 0.0)
    spread(width(1), SHORT, 4)
    back = back_conv(w1, width(0))
    for t in range(4):
        field[t, 0 : COLS * SHORT, :] = back[t]
    for t in range(4):
        for y in range(ROWS):
            out_ref[t, y] = field[t, pl.ds(y, COLS, SHORT), :].astype(BF16)


def per_device(latent, conv_one, conv_two, to_rgb, disc_one, disc_two, disc_head):
    x = latent[0]

    def widen(v, axis, dim):
        n = lax.axis_size(axis)
        size = v.shape[dim]
        before = lax.ppermute(
            lax.slice_in_dim(v, size - HALO, size, axis=dim), axis, [(i, (i + 1) % n) for i in range(n)]
        )
        after = lax.ppermute(
            lax.slice_in_dim(v, 0, HALO, axis=dim), axis, [((i + 1) % n, i) for i in range(n)]
        )
        return jnp.concatenate([before, v, after], dim)

    x = widen(x, "gx", 2)
    x = widen(x, "gy", 1)
    taps = lambda k: k.reshape(3, 9, *k.shape[3:])
    rgb_rows = jnp.swapaxes(to_rgb, 3, 4).reshape(81, 128).astype(F32)
    one_rows = jnp.pad(disc_one.reshape(81, 64).astype(F32), ((0, 0), (0, 64)))
    vmem = pl.BlockSpec(memory_space=pltpu.VMEM)
    hbm = pl.BlockSpec(memory_space=pl.ANY)
    p = WIDE * TALL + PAD
    out, logits = pl.pallas_call(
        kernel,
        out_shape=[
            jax.ShapeDtypeStruct((4, ROWS, COLS, 128), BF16),
            jax.ShapeDtypeStruct((COLS, ROWS, 128), F32),
        ],
        in_specs=[vmem, hbm, hbm, hbm, vmem, vmem, vmem],
        out_specs=[vmem, vmem],
        scratch_shapes=[
            pltpu.VMEM((4, p, 128), F32),
            pltpu.VMEM((4, p, 128), F32),
            pltpu.VMEM((4, p, 128), F32),
            pltpu.VMEM((2, p, 128), F32),
            pltpu.VMEM((3, p, 512), BF16),
            pltpu.VMEM((p, 128), F32),
            pltpu.VMEM((p, 128), F32),
            pltpu.VMEM((p, 128), F32),
            pltpu.VMEM((p, 128), F32),
        ]
        + [
            pltpu.VMEM((2, 9, 256, 256), BF16),
            pltpu.VMEM((2, 9, 256, 256), BF16),
            pltpu.VMEM((9, 256, 512), BF16),
            pltpu.VMEM((128, 512), F32),
            pltpu.VMEM((128, 512), BF16),
            pltpu.VMEM((128, 256), BF16),
            pltpu.SemaphoreType.DMA((24,)),
        ],
        compiler_params=pltpu.CompilerParams(vmem_limit_bytes=56 << 20),
    )(x, taps(conv_one), taps(conv_two), taps(disc_two), rgb_rows, one_rows, disc_head.reshape(1, 128))
    logits = jnp.transpose(logits[:, :, :4], (2, 1, 0)).astype(BF16)
    return out[None], logits[None]


def solution(mesh):
    placed = (P(None, None, "gy", "gx", None), P(), P(), P(), P(), P(), P())
    return jax.shard_map(
        per_device,
        mesh=mesh,
        in_specs=placed,
        out_specs=(P(None, None, "gy", "gx", None), P(None, None, "gy", "gx")),
        check_vma=False,
    )
```

```python
import jax
import jax.numpy as jnp
import numpy as np
from jax import lax
from jax.experimental import pallas as pl
from jax.experimental.pallas import tpu as pltpu
from jax.sharding import PartitionSpec as P

F32 = jnp.float32
BF16 = jnp.bfloat16

HALO = 10
ROWS, COLS = 24, 16
TALL = 48
SHORT = 32
WIDE = COLS + 2 * HALO
HIGH = ROWS + 2 * HALO
PAD = 256


def width(h):
    return COLS + 2 * h


def sigmoid(v):
    return 0.5 * jnp.tanh(0.5 * v) + 0.5


def silu(v):
    return v * sigmoid(v)


def dsilu(v):
    s = sigmoid(v)
    return s * (1.0 + v * (1.0 - s))


def lay_out(k1, k2, ks, rgb_rows, one_rows, w1, w2, sec, rgb_w, one_w, small, sems):
    loads = []
    for k, w in ((k1, w1), (k2, w2)):
        for far in range(2):
            for f in range(2):
                for t in range(2):
                    i = f - t + 2 - 2 * far
                    block = w.at[far, :, f * 128 : f * 128 + 128, t * 128 : t * 128 + 128]
                    if 0 <= i <= 2:
                        loads.append(pltpu.make_async_copy(k.at[i], block, sems.at[len(loads)]))
                    else:
                        block[...] = jnp.zeros(block.shape, BF16)
    for f in range(4):
        for t in range(4):
            i = f - t + 2
            block = sec.at[:, f * 64 : f * 64 + 64, t * 128 : t * 128 + 128]
            if 0 <= i <= 2:
                loads.append(pltpu.make_async_copy(ks.at[i], block, sems.at[len(loads)]))
            else:
                block[...] = jnp.zeros(block.shape, BF16)
    for c in loads:
        c.start()

    for rows, out, lanes, first in ((rgb_rows, rgb_w, 128, True), (one_rows, one_w, 64, False)):
        small[...] = jnp.zeros_like(small)
        for f in range(4):
            for t in range(4):
                i = (t - f if first else f - t) + 2
                if 0 <= i <= 2:
                    for n in range(9):
                        small[n * 12 + f * 3 : n * 12 + f * 3 + 3, t * lanes : t * lanes + lanes] = rows[
                            (i * 9 + n) * 3 : (i * 9 + n) * 3 + 3, 0:lanes
                        ]
        out[...] = small[:, 0 : 4 * lanes].astype(BF16)
    for c in loads:
        c.wait()


def kernel(
    own, left, right, top, bottom, w1_hbm, w2_hbm, sec_hbm, rgb_w, one_w, head,
    out_ref, logit_ref,
    field, pre1, pre2, pref, taps, valid, valid_s, part, pix, mid, line, w1, w2, sec, sems,
):
    loads = [
        pltpu.make_async_copy(a, b, sems.at[n])
        for n, (a, b) in enumerate(((w1_hbm, w1), (w2_hbm, w2), (sec_hbm, sec)))
    ]
    for c in loads:
        c.start()

    def arrived(which):
        loads[which].wait()

    gy, gx = lax.axis_index("gy"), lax.axis_index("gx")
    ny, nx = lax.axis_size("gy"), lax.axis_size("gx")

    def validity(ref, stride, h):
        first_x, first_y = gx * COLS - h, gy * ROWS - h
        y = first_y + lax.broadcasted_iota(jnp.int32, (stride, 128), 0)
        good_y = jnp.where((y >= 0) & (y < ny * ROWS), 1.0, 0.0).astype(F32)

        def body(x, _):
            place = first_x + x
            good_x = jnp.where((place >= 0) & (place < nx * COLS), 1.0, 0.0).astype(F32)
            ref[pl.ds(pl.multiple_of(x * stride, 8), stride), :] = good_y * good_x
            return 0

        lax.fori_loop(0, width(h), body, 0)

    validity(valid, TALL, HALO)
    validity(valid_s, SHORT, 2)

    def spread(count, stride, tiles, mask=None):
        step = 96

        def body(n, _):
            r = pl.multiple_of(n * step, 32)
            for j in range(3):
                good = None if mask is None else mask[pl.ds(r + j, step), :] > 0
                for t in range(tiles):
                    v = field[t, pl.ds(r + j, step), :]
                    if good is not None:
                        v = jnp.where(good, v, 0.0)
                    taps[j, pl.ds(r, step), t * 128 : t * 128 + 128] = v.astype(BF16)
            return 0

        lax.fori_loop(0, -(-count * stride // step), body, 0)

    def operand(base, rows, stride, tiles):
        return jnp.concatenate(
            [
                taps[j, pl.ds(pl.multiple_of(base + l * stride, 16), rows), tiles[0] * 128 : tiles[1] * 128]
                for j in range(3)
                for l in range(3)
            ],
            1,
        )

    def stack(w, rows=slice(None), lanes=slice(None)):
        v = w[:, rows, lanes]
        return v.reshape(-1, v.shape[-1])

    def across(w):
        return jnp.concatenate([w[8 - n] for n in range(9)], 1)

    def dot_t(a, b):
        return lax.dot_general(a, b, (((1,), (1,)), ((), ())), preferred_element_type=F32)

    def dot(a, b):
        return jnp.dot(a, b, preferred_element_type=F32)

    def place(ref, x, y, count):
        def body(n, _):
            for t in range(4):
                field[t, pl.ds(x * TALL + y + n, ref.shape[2], TALL), :] = ref[t, n].astype(F32)
            return 0

        lax.fori_loop(0, count, body, 0, unroll=2)

    place(left, 0, HALO, ROWS)
    place(own, HALO, HALO, ROWS)
    place(right, HALO + COLS, HALO, ROWS)
    place(top, 0, 0, HALO)
    place(bottom, 0, HALO + ROWS, HALO)
    spread(WIDE, TALL, 4, valid)

    def decode(w, pre, h, columns):
        rows = columns * TALL
        off = (HALO - h) * (TALL + 1)

        def body(n, _):
            base = pl.multiple_of(n * rows, 16)
            good = valid[pl.ds(base + off, rows), :] > 0
            near, far = operand(base, rows, TALL, (0, 2)), operand(base, rows, TALL, (2, 4))
            low = dot(near, stack(w.at[0]))
            high = dot(near, stack(w.at[1])) + dot(far, stack(w.at[0]))
            for t, (v, s) in enumerate(((low, 0), (low, 128), (high, 0), (high, 128))):
                v = v[:, s : s + 128]
                pre[t, pl.ds(base, rows), :] = v
                field[t, pl.ds(base, rows), :] = jnp.where(good, silu(v), 0.0)
            return 0

        lax.fori_loop(0, width(h) // columns, body, 0)

    arrived(0)
    decode(w1, pre1, 9, 17)
    spread(width(9), TALL, 4)
    arrived(1)
    decode(w2, pre2, 8, 16)

    def sum_columns(src, count, turn):
        rows = 6 * TALL

        def body(n, _):
            base = pl.multiple_of(n * rows, 8)
            total = None
            for l in range(3):
                v = src[pl.ds(base + l * TALL, rows), :]
                v = pltpu.roll(v, turn(l), 1) if turn(l) else v
                total = v if total is None else total + v
            mid[pl.ds(base, rows), :] = total
            return 0

        lax.fori_loop(0, -(-(count + 1) // 6), body, 0)

    def sum_rows(base, rows, turn):
        total = None
        for j in range(3):
            v = mid[pl.ds(base + j, rows), :]
            v = pltpu.roll(v, turn(j), 1) if turn(j) else v
            total = v if total is None else total + v
        return total

    def gather_taps(count, h, flip):
        off = (HALO - h) * (TALL + 1)
        turn = lambda size: lambda n: (128 - size * (2 - n if flip else n)) % 128
        sum_columns(part, count, turn(12))
        rows = 6 * TALL
        lane = lax.broadcasted_iota(jnp.int32, (rows, 128), 1)

        def body(n, _):
            base = pl.multiple_of(n * rows, 8)
            total = sum_rows(base, rows, turn(36))
            good = (valid[pl.ds(base + off, rows), :] > 0) & (lane < 12)
            pix[pl.ds(base, rows), :] = jnp.where(good, total, 0.0).astype(BF16).astype(F32)
            return 0

        lax.fori_loop(0, -(-count // 6), body, 0)

    def scatter_taps(count, stride, flip):
        turn = lambda size: lambda n: size * (2 - n if flip else n)
        sum_columns(pix, count, turn(12))

        def body(n, _):
            for c in range(4):
                x = n * 4 + c
                v = sum_rows(pl.multiple_of(x * TALL, 8), stride, turn(36))
                taps[0, pl.ds(pl.multiple_of(x * stride, 16), stride), 0:128] = v.astype(BF16)
            return 0

        lax.fori_loop(0, count // 4, body, 0)

    def rgb_part(n, _):
        rows = 16 * TALL
        base = pl.multiple_of(n * rows, 16)
        a = jnp.concatenate([field[t, pl.ds(base, rows), :].astype(BF16) for t in range(4)], 1)
        part[pl.ds(base, rows), :] = dot_t(a, rgb_w[...])
        return 0

    lax.fori_loop(0, width(8) // 16, rgb_part, 0)
    gather_taps(width(7), 7, False)

    scatter_taps(width(6), TALL, False)

    def first(n, _):
        rows = 14 * TALL
        base = pl.multiple_of(n * rows, 16)
        good = valid[pl.ds(base + 4 * (TALL + 1), rows), :] > 0
        v = dot(taps[0, pl.ds(base, rows), 0:128], one_w[...])
        for t in range(2):
            p = v[:, t * 128 : t * 128 + 128]
            pref[t, pl.ds(base, rows), :] = p
            field[t, pl.ds(base, rows), :] = jnp.where(good, silu(p), 0.0)
        return 0

    lax.fori_loop(0, 2, first, 0)
    spread(width(6), TALL, 2)
    arrived(2)

    def second(n, _):
        rows = 13 * TALL
        base = pl.multiple_of(n * rows, 16)
        good = valid[pl.ds(base + 5 * (TALL + 1), rows), :] > 0
        low = dot(operand(base, rows, TALL, (0, 1)), stack(sec, slice(0, 128), slice(0, 256)))
        high = dot(operand(base, rows, TALL, (0, 2)), stack(sec, slice(None), slice(256, 512)))
        lane = lax.broadcasted_iota(jnp.int32, (rows, 128), 1)
        logits = jnp.zeros((rows, 128), F32)
        for t, (v, s) in enumerate(((low, 0), (low, 128), (high, 0), (high, 128))):
            v = v[:, s : s + 128]
            sg = sigmoid(v)
            score = jnp.sum(v * sg * head[...], axis=1, keepdims=True)
            push = -sigmoid(-score)
            logits = jnp.where(lane == t, score, logits)
            g = push * head[...] * (sg * (1.0 + v * (1.0 - sg)))
            field[t, pl.ds(base, rows), :] = jnp.where(good, g, 0.0)
        part[pl.ds(base, rows), :] = logits
        return 0

    lax.fori_loop(0, 2, second, 0)
    pick = jnp.where(
        lax.broadcasted_iota(jnp.int32, (16, 128), 0) == lax.broadcasted_iota(jnp.int32, (16, 128), 1), 1.0, 0.0
    ).astype(BF16)
    for x in range(COLS):
        v = dot_t(pick, part[pl.ds((x + 5) * TALL + 5, 128), :].astype(BF16))
        for t in range(4):
            line[t, x : x + 1, :] = v[t : t + 1]
    logit_ref[...] = line[:, :, 0:ROWS].astype(BF16)
    spread(width(5), TALL, 4)

    def second_back(n, _):
        rows = 12 * TALL
        base = pl.multiple_of(n * rows, 16)
        good = valid[pl.ds(base + 6 * (TALL + 1), rows), :] > 0
        v = dot_t(operand(base, rows, TALL, (0, 4)), across(sec))
        g = []
        for t in range(2):
            p = pref[t, pl.ds(base + 2 * (TALL + 1), rows), :]
            g.append(jnp.where(good, v[:, t * 128 : t * 128 + 128] * dsilu(p), 0.0).astype(BF16))
        part[pl.ds(base, rows), :] = dot_t(jnp.concatenate(g, 1), one_w[...])
        return 0

    lax.fori_loop(0, 2, second_back, 0)
    gather_taps(width(3), 3, True)

    scatter_taps(width(2), SHORT, True)
    back = dot(taps[0, 0 : width(2) * SHORT, 0:128], rgb_w[...])
    for t in range(4):
        for x in range(width(2)):
            p = pre2[t, pl.ds((x + 6) * TALL + 6, SHORT), :]
            g = back[x * SHORT : (x + 1) * SHORT, t * 128 : t * 128 + 128] * dsilu(p)
            good = valid_s[pl.ds(x * SHORT, SHORT), :] > 0
            field[t, pl.ds(x * SHORT, SHORT), :] = jnp.where(good, g, 0.0)
    spread(width(2), SHORT, 4)

    def back_conv(w, count):
        rows = count * SHORT
        near, far = operand(0, rows, SHORT, (0, 2)), operand(0, rows, SHORT, (2, 4))
        high = dot_t(far, across(w.at[0]))
        low = dot_t(far, across(w.at[1])) + dot_t(near, across(w.at[0]))
        return [v[:, s : s + 128] for v in (low, high) for s in (0, 128)]

    back = back_conv(w2, width(1))
    for t in range(4):
        for x in range(width(1)):
            p = pre1[t, pl.ds((x + 8) * TALL + 8, SHORT), :]
            g = back[t][x * SHORT : (x + 1) * SHORT] * dsilu(p)
            good = valid_s[pl.ds((x + 1) * SHORT + 1, SHORT), :] > 0
            field[t, pl.ds(x * SHORT, SHORT), :] = jnp.where(good, g, 0.0)
    spread(width(1), SHORT, 4)
    back = back_conv(w1, width(0))
    for t in range(4):
        field[t, 0 : COLS * SHORT, :] = back[t]
    for t in range(4):
        for y in range(ROWS):
            out_ref[t, y] = field[t, pl.ds(y, COLS, SHORT), :].astype(BF16)


def per_device(latent, conv_one, conv_two, to_rgb, disc_one, disc_two, disc_head):
    x = latent[0]

    def sides(v, axis, dim):
        n = lax.axis_size(axis)
        size = v.shape[dim]
        before = lax.ppermute(
            lax.slice_in_dim(v, size - HALO, size, axis=dim), axis, [(i, (i + 1) % n) for i in range(n)]
        )
        after = lax.ppermute(
            lax.slice_in_dim(v, 0, HALO, axis=dim), axis, [((i + 1) % n, i) for i in range(n)]
        )
        return before, after

    left, right = sides(x, "gx", 2)
    top, bottom = sides(jnp.concatenate([left, x, right], 2), "gy", 1)
    taps = lambda k: k.reshape(3, 9, *k.shape[3:])
    rgb_rows = jnp.swapaxes(to_rgb, 3, 4).reshape(81, 128).astype(F32)
    one_rows = jnp.pad(disc_one.reshape(81, 64).astype(F32), ((0, 0), (0, 64)))
    vmem = pl.BlockSpec(memory_space=pltpu.VMEM)
    hbm = pl.BlockSpec(memory_space=pl.ANY)
    p = WIDE * TALL + PAD
    shapes = [(2, 9, 256, 256), (2, 9, 256, 256), (9, 256, 512), (128, 512), (128, 256)]
    weights = pl.pallas_call(
        lay_out,
        out_shape=[jax.ShapeDtypeStruct(n, BF16) for n in shapes],
        in_specs=[hbm, hbm, hbm, vmem, vmem],
        out_specs=[vmem] * 5,
        scratch_shapes=[pltpu.VMEM((128, 512), F32), pltpu.SemaphoreType.DMA((24,))],
        compiler_params=pltpu.CompilerParams(vmem_limit_bytes=16 << 20),
        cost_estimate=pl.CostEstimate(flops=0, bytes_accessed=12 << 20, transcendentals=0),
    )(taps(conv_one), taps(conv_two), taps(disc_two), rgb_rows, one_rows)
    out, logits = pl.pallas_call(
        kernel,
        out_shape=[
            jax.ShapeDtypeStruct((4, ROWS, COLS, 128), BF16),
            jax.ShapeDtypeStruct((4, COLS, ROWS), BF16),
        ],
        in_specs=[vmem] * 5 + [hbm] * 3 + [vmem] * 3,
        out_specs=[vmem, vmem],
        scratch_shapes=[
            pltpu.VMEM((4, p, 128), F32),
            pltpu.VMEM((4, p, 128), F32),
            pltpu.VMEM((4, p, 128), F32),
            pltpu.VMEM((2, p, 128), F32),
            pltpu.VMEM((3, p, 512), BF16),
            pltpu.VMEM((p, 128), F32),
            pltpu.VMEM((p, 128), F32),
            pltpu.VMEM((p, 128), F32),
            pltpu.VMEM((p, 128), F32),
            pltpu.VMEM((p, 128), F32),
            pltpu.VMEM((4, COLS, 128), F32),
        ]
        + [pltpu.VMEM(n, BF16) for n in shapes[:3]]
        + [pltpu.SemaphoreType.DMA((3,))],
        compiler_params=pltpu.CompilerParams(vmem_limit_bytes=56 << 20),
    )(x, left, right, top, bottom, *weights, disc_head.reshape(1, 128))
    return out[None], jnp.swapaxes(logits, 1, 2)[None]


def solution(mesh):
    placed = (P(None, None, "gy", "gx", None), P(), P(), P(), P(), P(), P())
    return jax.shard_map(
        per_device,
        mesh=mesh,
        in_specs=placed,
        out_specs=(P(None, None, "gy", "gx", None), P(None, None, "gy", "gx")),
        check_vma=False,
    )
```

```python
import jax
import jax.numpy as jnp
import numpy as np
from jax import lax
from jax.experimental import pallas as pl
from jax.experimental.pallas import tpu as pltpu
from jax.sharding import PartitionSpec as P

F32 = jnp.float32
BF16 = jnp.bfloat16

HALO = 10
ROWS, COLS = 24, 16
TALL = 48
SHORT = 32
WIDE = COLS + 2 * HALO
HIGH = ROWS + 2 * HALO
PAD = 256


def width(h):
    return COLS + 2 * h


def sigmoid(v):
    return 0.5 * jnp.tanh(0.5 * v) + 0.5


def silu(v):
    return v * sigmoid(v)


def dsilu(v):
    s = sigmoid(v)
    return s * (1.0 + v * (1.0 - s))


def lay_out(k1, k2, ks, rgb_rows, one_rows, w1, w2, sec, rgb_w, one_w, small, sems):
    loads = []
    for k, w in ((k1, w1), (k2, w2)):
        for far in range(2):
            for f in range(2):
                for t in range(2):
                    i = f - t + 2 - 2 * far
                    block = w.at[far, :, f * 128 : f * 128 + 128, t * 128 : t * 128 + 128]
                    if 0 <= i <= 2:
                        loads.append(pltpu.make_async_copy(k.at[i], block, sems.at[len(loads)]))
                    else:
                        block[...] = jnp.zeros(block.shape, BF16)
    for f in range(4):
        for t in range(4):
            i = f - t + 2
            block = sec.at[:, f * 64 : f * 64 + 64, t * 128 : t * 128 + 128]
            if 0 <= i <= 2:
                loads.append(pltpu.make_async_copy(ks.at[i], block, sems.at[len(loads)]))
            else:
                block[...] = jnp.zeros(block.shape, BF16)
    for c in loads:
        c.start()

    for rows, out, lanes, first in ((rgb_rows, rgb_w, 128, True), (one_rows, one_w, 64, False)):
        small[...] = jnp.zeros_like(small)
        for f in range(4):
            for t in range(4):
                i = (t - f if first else f - t) + 2
                if 0 <= i <= 2:
                    for n in range(9):
                        small[n * 12 + f * 3 : n * 12 + f * 3 + 3, t * lanes : t * lanes + lanes] = rows[
                            (i * 9 + n) * 3 : (i * 9 + n) * 3 + 3, 0:lanes
                        ]
        out[...] = small[:, 0 : 4 * lanes].astype(BF16)
    for c in loads:
        c.wait()


def cut_columns(own, first, last, rows):
    for t in range(4):
        rows[t] = own[t].reshape(ROWS * COLS, 128).astype(F32)
    for x in range(HALO):
        for t in range(4):
            first[x, t] = rows[t, pl.ds(x, ROWS, COLS), :].astype(BF16)
            last[x, t] = rows[t, pl.ds(COLS - HALO + x, ROWS, COLS), :].astype(BF16)


def cut_rows(own, left, right, first, last, rows):
    low = ROWS - HALO
    for t in range(4):
        for y in range(HALO):
            rows[0, t, pl.ds(HALO * HALO + y, COLS, HALO), :] = own[t, y].astype(F32)
            rows[1, t, pl.ds(HALO * HALO + y, COLS, HALO), :] = own[t, low + y].astype(F32)
        for ref, start in ((left, 0), (right, HALO + COLS)):
            for x in range(HALO):
                v = ref[x, t].astype(F32)
                at = (start + x) * HALO
                rows[0, t, at : at + HALO, :] = v[0:HALO]
                rows[1, t, at : at + HALO, :] = v[low:ROWS]
        first[t] = rows[0, t].astype(BF16)
        last[t] = rows[1, t].astype(BF16)


def kernel(
    own, left, right, top, bottom, w1, w2, sec, rgb_w, one_w, head,
    out_ref, logit_ref,
    field, pre1, pre2, pref, taps, valid, valid_s, part, pix, mid, line, edge,
):
    gy, gx = lax.axis_index("gy"), lax.axis_index("gx")
    ny, nx = lax.axis_size("gy"), lax.axis_size("gx")

    def validity(ref, stride, h):
        first_x, first_y = gx * COLS - h, gy * ROWS - h
        y = first_y + lax.broadcasted_iota(jnp.int32, (stride, 128), 0)
        good_y = jnp.where((y >= 0) & (y < ny * ROWS), 1.0, 0.0).astype(F32)

        def body(x, _):
            place = first_x + x
            good_x = jnp.where((place >= 0) & (place < nx * COLS), 1.0, 0.0).astype(F32)
            ref[pl.ds(pl.multiple_of(x * stride, 8), stride), :] = good_y * good_x
            return 0

        lax.fori_loop(0, width(h), body, 0)

    validity(valid, TALL, HALO)
    validity(valid_s, SHORT, 2)

    def spread(count, stride, tiles, mask=None):
        step = 96

        def body(n, _):
            r = pl.multiple_of(n * step, 32)
            for j in range(3):
                good = None if mask is None else mask[pl.ds(r + j, step), :] > 0
                for t in range(tiles):
                    v = field[t, pl.ds(r + j, step), :]
                    if good is not None:
                        v = jnp.where(good, v, 0.0)
                    taps[j, pl.ds(r, step), t * 128 : t * 128 + 128] = v.astype(BF16)
            return 0

        lax.fori_loop(0, -(-count * stride // step), body, 0)

    def operand(base, rows, stride, tiles):
        return jnp.concatenate(
            [
                taps[j, pl.ds(pl.multiple_of(base + l * stride, 16), rows), tiles[0] * 128 : tiles[1] * 128]
                for j in range(3)
                for l in range(3)
            ],
            1,
        )

    def stack(w, rows=slice(None), lanes=slice(None)):
        v = w[:, rows, lanes]
        return v.reshape(-1, v.shape[-1])

    def across(w):
        return jnp.concatenate([w[8 - n] for n in range(9)], 1)

    def dot_t(a, b):
        return lax.dot_general(a, b, (((1,), (1,)), ((), ())), preferred_element_type=F32)

    def dot(a, b):
        return jnp.dot(a, b, preferred_element_type=F32)

    def place(n, _):
        for t in range(4):
            field[t, pl.ds(HALO * TALL + HALO + n, COLS, TALL), :] = own[t, n].astype(F32)
        return 0

    lax.fori_loop(0, ROWS, place, 0, unroll=4)
    for t in range(4):
        for x in range(HALO):
            for ref, start in ((left, 0), (right, HALO + COLS)):
                at = (start + x) * TALL + HALO
                field[t, at : at + ROWS, :] = ref[x, t].astype(F32)
        for n, (ref, y) in enumerate(((top, 0), (bottom, HALO + ROWS))):
            edge[n, t] = ref[t].astype(F32)
            for x in range(WIDE):
                field[t, x * TALL + y : x * TALL + y + HALO, :] = edge[n, t, x * HALO : x * HALO + HALO, :]
    spread(WIDE, TALL, 4, valid)

    def decode(w, pre, h, columns):
        rows = columns * TALL
        off = (HALO - h) * (TALL + 1)

        def body(n, _):
            base = pl.multiple_of(n * rows, 16)
            good = valid[pl.ds(base + off, rows), :] > 0
            near, far = operand(base, rows, TALL, (0, 2)), operand(base, rows, TALL, (2, 4))
            low = dot(near, stack(w.at[0]))
            high = dot(near, stack(w.at[1])) + dot(far, stack(w.at[0]))
            for t, (v, s) in enumerate(((low, 0), (low, 128), (high, 0), (high, 128))):
                v = v[:, s : s + 128]
                pre[t, pl.ds(base, rows), :] = v
                field[t, pl.ds(base, rows), :] = jnp.where(good, silu(v), 0.0)
            return 0

        lax.fori_loop(0, width(h) // columns, body, 0)

    decode(w1, pre1, 9, 17)
    spread(width(9), TALL, 4)
    decode(w2, pre2, 8, 16)

    def sum_columns(src, count, turn):
        rows = 6 * TALL

        def body(n, _):
            base = pl.multiple_of(n * rows, 8)
            total = None
            for l in range(3):
                v = src[pl.ds(base + l * TALL, rows), :]
                v = pltpu.roll(v, turn(l), 1) if turn(l) else v
                total = v if total is None else total + v
            mid[pl.ds(base, rows), :] = total
            return 0

        lax.fori_loop(0, -(-(count + 1) // 6), body, 0)

    def sum_rows(base, rows, turn):
        total = None
        for j in range(3):
            v = mid[pl.ds(base + j, rows), :]
            v = pltpu.roll(v, turn(j), 1) if turn(j) else v
            total = v if total is None else total + v
        return total

    def gather_taps(count, h, flip):
        off = (HALO - h) * (TALL + 1)
        turn = lambda size: lambda n: (128 - size * (2 - n if flip else n)) % 128
        sum_columns(part, count, turn(12))
        rows = 6 * TALL
        lane = lax.broadcasted_iota(jnp.int32, (rows, 128), 1)

        def body(n, _):
            base = pl.multiple_of(n * rows, 8)
            total = sum_rows(base, rows, turn(36))
            good = (valid[pl.ds(base + off, rows), :] > 0) & (lane < 12)
            pix[pl.ds(base, rows), :] = jnp.where(good, total, 0.0).astype(BF16).astype(F32)
            return 0

        lax.fori_loop(0, -(-count // 6), body, 0)

    def scatter_taps(count, stride, flip):
        turn = lambda size: lambda n: size * (2 - n if flip else n)
        sum_columns(pix, count, turn(12))

        def body(n, _):
            for c in range(4):
                x = n * 4 + c
                v = sum_rows(pl.multiple_of(x * TALL, 8), stride, turn(36))
                taps[0, pl.ds(pl.multiple_of(x * stride, 16), stride), 0:128] = v.astype(BF16)
            return 0

        lax.fori_loop(0, count // 4, body, 0)

    def rgb_part(n, _):
        rows = 16 * TALL
        base = pl.multiple_of(n * rows, 16)
        a = jnp.concatenate([field[t, pl.ds(base, rows), :].astype(BF16) for t in range(4)], 1)
        part[pl.ds(base, rows), :] = dot_t(a, rgb_w[...])
        return 0

    lax.fori_loop(0, width(8) // 16, rgb_part, 0)
    gather_taps(width(7), 7, False)

    scatter_taps(width(6), TALL, False)

    def first(n, _):
        rows = 14 * TALL
        base = pl.multiple_of(n * rows, 16)
        good = valid[pl.ds(base + 4 * (TALL + 1), rows), :] > 0
        v = dot(taps[0, pl.ds(base, rows), 0:128], one_w[...])
        for t in range(2):
            p = v[:, t * 128 : t * 128 + 128]
            pref[t, pl.ds(base, rows), :] = p
            field[t, pl.ds(base, rows), :] = jnp.where(good, silu(p), 0.0)
        return 0

    lax.fori_loop(0, 2, first, 0)
    spread(width(6), TALL, 2)

    def second(n, _):
        rows = 13 * TALL
        base = pl.multiple_of(n * rows, 16)
        good = valid[pl.ds(base + 5 * (TALL + 1), rows), :] > 0
        low = dot(operand(base, rows, TALL, (0, 1)), stack(sec, slice(0, 128), slice(0, 256)))
        high = dot(operand(base, rows, TALL, (0, 2)), stack(sec, slice(None), slice(256, 512)))
        lane = lax.broadcasted_iota(jnp.int32, (rows, 128), 1)
        logits = jnp.zeros((rows, 128), F32)
        for t, (v, s) in enumerate(((low, 0), (low, 128), (high, 0), (high, 128))):
            v = v[:, s : s + 128]
            sg = sigmoid(v)
            score = jnp.sum(v * sg * head[...], axis=1, keepdims=True)
            push = -sigmoid(-score)
            logits = jnp.where(lane == t, score, logits)
            g = push * head[...] * (sg * (1.0 + v * (1.0 - sg)))
            field[t, pl.ds(base, rows), :] = jnp.where(good, g, 0.0)
        part[pl.ds(base, rows), :] = logits
        return 0

    lax.fori_loop(0, 2, second, 0)
    pick = jnp.where(
        lax.broadcasted_iota(jnp.int32, (16, 128), 0) == lax.broadcasted_iota(jnp.int32, (16, 128), 1), 1.0, 0.0
    ).astype(BF16)
    for x in range(COLS):
        v = dot_t(pick, part[pl.ds((x + 5) * TALL + 5, 128), :].astype(BF16))
        for t in range(4):
            line[t, x : x + 1, :] = v[t : t + 1]
    logit_ref[...] = line[:, :, 0:ROWS].astype(BF16)
    spread(width(5), TALL, 4)

    def second_back(n, _):
        rows = 12 * TALL
        base = pl.multiple_of(n * rows, 16)
        good = valid[pl.ds(base + 6 * (TALL + 1), rows), :] > 0
        v = dot_t(operand(base, rows, TALL, (0, 4)), across(sec))
        g = []
        for t in range(2):
            p = pref[t, pl.ds(base + 2 * (TALL + 1), rows), :]
            g.append(jnp.where(good, v[:, t * 128 : t * 128 + 128] * dsilu(p), 0.0).astype(BF16))
        part[pl.ds(base, rows), :] = dot_t(jnp.concatenate(g, 1), one_w[...])
        return 0

    lax.fori_loop(0, 2, second_back, 0)
    gather_taps(width(3), 3, True)

    scatter_taps(width(2), SHORT, True)
    back = dot(taps[0, 0 : width(2) * SHORT, 0:128], rgb_w[...])
    for t in range(4):
        for x in range(width(2)):
            p = pre2[t, pl.ds((x + 6) * TALL + 6, SHORT), :]
            g = back[x * SHORT : (x + 1) * SHORT, t * 128 : t * 128 + 128] * dsilu(p)
            good = valid_s[pl.ds(x * SHORT, SHORT), :] > 0
            field[t, pl.ds(x * SHORT, SHORT), :] = jnp.where(good, g, 0.0)
    spread(width(2), SHORT, 4)

    def back_conv(w, count):
        rows = count * SHORT
        near, far = operand(0, rows, SHORT, (0, 2)), operand(0, rows, SHORT, (2, 4))
        high = dot_t(far, across(w.at[0]))
        low = dot_t(far, across(w.at[1])) + dot_t(near, across(w.at[0]))
        return [v[:, s : s + 128] for v in (low, high) for s in (0, 128)]

    back = back_conv(w2, width(1))
    for t in range(4):
        for x in range(width(1)):
            p = pre1[t, pl.ds((x + 8) * TALL + 8, SHORT), :]
            g = back[t][x * SHORT : (x + 1) * SHORT] * dsilu(p)
            good = valid_s[pl.ds((x + 1) * SHORT + 1, SHORT), :] > 0
            field[t, pl.ds(x * SHORT, SHORT), :] = jnp.where(good, g, 0.0)
    spread(width(1), SHORT, 4)
    back = back_conv(w1, width(0))
    for t in range(4):
        field[t, 0 : COLS * SHORT, :] = back[t]
    for t in range(4):
        for y in range(ROWS):
            out_ref[t, y] = field[t, pl.ds(y, COLS, SHORT), :].astype(BF16)


def per_device(latent, conv_one, conv_two, to_rgb, disc_one, disc_two, disc_head):
    x = latent[0]

    vmem = pl.BlockSpec(memory_space=pltpu.VMEM)
    hbm = pl.BlockSpec(memory_space=pl.ANY)

    def exchange(first, last, axis):
        n = lax.axis_size(axis)
        before = lax.ppermute(last, axis, [(i, (i + 1) % n) for i in range(n)])
        after = lax.ppermute(first, axis, [((i + 1) % n, i) for i in range(n)])
        return before, after

    first, last = pl.pallas_call(
        cut_columns,
        out_shape=[jax.ShapeDtypeStruct((HALO, 4, ROWS, 128), BF16)] * 2,
        in_specs=[vmem],
        out_specs=[vmem] * 2,
        scratch_shapes=[pltpu.VMEM((4, ROWS * COLS, 128), F32)],
        compiler_params=pltpu.CompilerParams(vmem_limit_bytes=8 << 20),
    )(x)
    left, right = exchange(first, last, "gx")
    first, last = pl.pallas_call(
        cut_rows,
        out_shape=[jax.ShapeDtypeStruct((4, WIDE * HALO, 128), BF16)] * 2,
        in_specs=[vmem] * 3,
        out_specs=[vmem] * 2,
        scratch_shapes=[pltpu.VMEM((2, 4, WIDE * HALO, 128), F32)],
        compiler_params=pltpu.CompilerParams(vmem_limit_bytes=8 << 20),
    )(x, left, right)
    top, bottom = exchange(first, last, "gy")
    taps = lambda k: k.reshape(3, 9, *k.shape[3:])
    rgb_rows = jnp.swapaxes(to_rgb, 3, 4).reshape(81, 128).astype(F32)
    one_rows = jnp.pad(disc_one.reshape(81, 64).astype(F32), ((0, 0), (0, 64)))
    p = WIDE * TALL + PAD
    shapes = [(2, 9, 256, 256), (2, 9, 256, 256), (9, 256, 512), (128, 512), (128, 256)]
    weights = pl.pallas_call(
        lay_out,
        out_shape=[jax.ShapeDtypeStruct(n, BF16) for n in shapes],
        in_specs=[hbm, hbm, hbm, vmem, vmem],
        out_specs=[vmem] * 5,
        scratch_shapes=[pltpu.VMEM((128, 512), F32), pltpu.SemaphoreType.DMA((24,))],
        compiler_params=pltpu.CompilerParams(vmem_limit_bytes=16 << 20),
        cost_estimate=pl.CostEstimate(flops=0, bytes_accessed=12 << 20, transcendentals=0),
    )(taps(conv_one), taps(conv_two), taps(disc_two), rgb_rows, one_rows)
    out, logits = pl.pallas_call(
        kernel,
        out_shape=[
            jax.ShapeDtypeStruct((4, ROWS, COLS, 128), BF16),
            jax.ShapeDtypeStruct((4, COLS, ROWS), BF16),
        ],
        in_specs=[vmem] * 11,
        out_specs=[vmem, vmem],
        scratch_shapes=[
            pltpu.VMEM((4, p, 128), F32),
            pltpu.VMEM((4, p, 128), F32),
            pltpu.VMEM((4, p, 128), F32),
            pltpu.VMEM((2, p, 128), F32),
            pltpu.VMEM((3, p, 512), BF16),
            pltpu.VMEM((p, 128), F32),
            pltpu.VMEM((p, 128), F32),
            pltpu.VMEM((p, 128), F32),
            pltpu.VMEM((p, 128), F32),
            pltpu.VMEM((p, 128), F32),
            pltpu.VMEM((4, COLS, 128), F32),
            pltpu.VMEM((2, 4, WIDE * HALO, 128), F32),
        ],
        compiler_params=pltpu.CompilerParams(vmem_limit_bytes=34 << 20),
    )(x, left, right, top, bottom, *weights, disc_head.reshape(1, 128))
    return out[None], jnp.swapaxes(logits, 1, 2)[None]


def solution(mesh):
    placed = (P(None, None, "gy", "gx", None), P(), P(), P(), P(), P(), P())
    return jax.shard_map(
        per_device,
        mesh=mesh,
        in_specs=placed,
        out_specs=(P(None, None, "gy", "gx", None), P(None, None, "gy", "gx")),
        check_vma=False,
    )
```

```python
import jax
import jax.numpy as jnp
import numpy as np
from jax import lax
from jax.experimental import pallas as pl
from jax.experimental.pallas import tpu as pltpu
from jax.sharding import PartitionSpec as P

F32 = jnp.float32
BF16 = jnp.bfloat16

HALO = 10
ROWS, COLS = 24, 16
TALL = 48
SHORT = 32
WIDE = COLS + 2 * HALO
HIGH = ROWS + 2 * HALO
PAD = 256


def width(h):
    return COLS + 2 * h


def sigmoid(v):
    return 0.5 * jnp.tanh(0.5 * v) + 0.5


def silu(v):
    half = 0.5 * v
    return half + half * jnp.tanh(half)


def dsilu(v):
    s = sigmoid(v)
    return s * (1.0 + v * (1.0 - s))


def lay_out(k1, k2, ks, rgb_rows, one_rows, w1, w2, sec, rgb_w, one_w, rgb_taps, one_taps, small, sems):
    loads = []
    for k, w in ((k1, w1), (k2, w2)):
        for far in range(2):
            for f in range(2):
                for t in range(2):
                    i = f - t + 2 - 2 * far
                    block = w.at[far, :, f * 128 : f * 128 + 128, t * 128 : t * 128 + 128]
                    if 0 <= i <= 2:
                        loads.append(pltpu.make_async_copy(k.at[i], block, sems.at[len(loads)]))
                    else:
                        block[...] = jnp.zeros(block.shape, BF16)
    for f in range(4):
        for t in range(4):
            i = f - t + 2
            block = sec.at[:, f * 64 : f * 64 + 64, t * 128 : t * 128 + 128]
            if 0 <= i <= 2:
                loads.append(pltpu.make_async_copy(ks.at[i], block, sems.at[len(loads)]))
            else:
                block[...] = jnp.zeros(block.shape, BF16)
    for c in loads:
        c.start()

    mine = lax.broadcasted_iota(jnp.int32, (16, 1), 0) < 12
    for rows, out, each, lanes, first in (
        (rgb_rows, rgb_w, rgb_taps, 128, True),
        (one_rows, one_w, one_taps, 64, False),
    ):
        small[...] = jnp.zeros_like(small)
        for f in range(4):
            for t in range(4):
                i = (t - f if first else f - t) + 2
                if 0 <= i <= 2:
                    for n in range(9):
                        small[n * 12 + f * 3 : n * 12 + f * 3 + 3, t * lanes : t * lanes + lanes] = rows[
                            (i * 9 + n) * 3 : (i * 9 + n) * 3 + 3, 0:lanes
                        ]
        out[...] = small[:, 0 : 4 * lanes].astype(BF16)
        each[...] = jnp.zeros_like(each)
        for n in range(9):
            v = small[n * 12 : n * 12 + 16, 0 : 4 * lanes]
            each[n, 0:16] = jnp.where(mine, v, 0.0).astype(BF16)
    for c in loads:
        c.wait()


def cut_columns(own, first, last, rows):
    for t in range(4):
        rows[t] = own[t].reshape(ROWS * COLS, 128).astype(F32)
    for x in range(HALO):
        for t in range(4):
            first[x, t] = rows[t, pl.ds(x, ROWS, COLS), :].astype(BF16)
            last[x, t] = rows[t, pl.ds(COLS - HALO + x, ROWS, COLS), :].astype(BF16)


def cut_rows(own, left, right, first, last, rows):
    low = ROWS - HALO
    gx, nx = lax.axis_index("gx"), lax.axis_size("gx")
    inside = (jnp.where(gx > 0, 1.0, 0.0).astype(F32), jnp.where(gx < nx - 1, 1.0, 0.0).astype(F32))
    for t in range(4):
        for y in range(HALO):
            rows[0, t, pl.ds(HALO * HALO + y, COLS, HALO), :] = own[t, y].astype(F32)
            rows[1, t, pl.ds(HALO * HALO + y, COLS, HALO), :] = own[t, low + y].astype(F32)
        for ref, start, good in ((left, 0, inside[0]), (right, HALO + COLS, inside[1])):
            for x in range(HALO):
                v = ref[x, t].astype(F32) * good
                at = (start + x) * HALO
                rows[0, t, at : at + HALO, :] = v[0:HALO]
                rows[1, t, at : at + HALO, :] = v[low:ROWS]
        first[t] = rows[0, t].astype(BF16)
        last[t] = rows[1, t].astype(BF16)


def kernel(
    own, left, right, top, bottom, w1, w2, sec, rgb_w, one_w, rgb_taps, one_taps, head,
    out_ref, logit_ref,
    field, pre1, pre2, pref, taps, valid, valid_s, part, pix, mid, line, edge,
):
    gy, gx = lax.axis_index("gy"), lax.axis_index("gx")
    ny, nx = lax.axis_size("gy"), lax.axis_size("gx")

    def validity(ref, stride, h):
        first_x, first_y = gx * COLS - h, gy * ROWS - h
        y = first_y + lax.broadcasted_iota(jnp.int32, (stride, 128), 0)
        good_y = jnp.where((y >= 0) & (y < ny * ROWS), 1.0, 0.0).astype(F32)

        def body(x, _):
            place = first_x + x
            good_x = jnp.where((place >= 0) & (place < nx * COLS), 1.0, 0.0).astype(F32)
            ref[pl.ds(pl.multiple_of(x * stride, 8), stride), :] = good_y * good_x
            return 0

        lax.fori_loop(0, width(h), body, 0)

    validity(valid, TALL, HALO)
    validity(valid_s, SHORT, 2)

    def spread(count, stride, tiles, source=None):
        step = 96

        def body(n, _):
            r = pl.multiple_of(n * step, 32)
            for j in range(3):
                for t in range(tiles):
                    v = field[t, pl.ds(r + j, step), :] if source is None else source[pl.ds(r + j, step), :]
                    taps[j, pl.ds(r, step), t * 128 : t * 128 + 128] = v.astype(BF16)
            return 0

        lax.fori_loop(0, -(-count * stride // step), body, 0)

    def operand(base, rows, stride, tiles):
        return jnp.concatenate(
            [
                taps[j, pl.ds(pl.multiple_of(base + l * stride, 16), rows), tiles[0] * 128 : tiles[1] * 128]
                for j in range(3)
                for l in range(3)
            ],
            1,
        )

    def stack(w, rows=slice(None), lanes=slice(None)):
        v = w[:, rows, lanes]
        return v.reshape(-1, v.shape[-1])

    def across(w):
        return jnp.concatenate([w[8 - n] for n in range(9)], 1)

    def dot_t(a, b):
        return lax.dot_general(a, b, (((1,), (1,)), ((), ())), preferred_element_type=F32)

    def dot(a, b):
        return jnp.dot(a, b, preferred_element_type=F32)

    def place(n, _):
        for t in range(4):
            field[t, pl.ds(HALO * TALL + HALO + n, COLS, TALL), :] = own[t, n].astype(F32)
        return 0

    lax.fori_loop(0, ROWS, place, 0, unroll=4)
    one = lambda test: jnp.where(test, 1.0, 0.0).astype(F32)
    for t in range(4):
        for x in range(HALO):
            for ref, start, good in ((left, 0, one(gx > 0)), (right, HALO + COLS, one(gx < nx - 1))):
                at = (start + x) * TALL + HALO
                field[t, at : at + ROWS, :] = ref[x, t].astype(F32) * good
        for n, (ref, y, good) in enumerate(((top, 0, one(gy > 0)), (bottom, HALO + ROWS, one(gy < ny - 1)))):
            edge[n, t] = ref[t].astype(F32) * good
            for x in range(WIDE):
                field[t, x * TALL + y : x * TALL + y + HALO, :] = edge[n, t, x * HALO : x * HALO + HALO, :]
    spread(WIDE, TALL, 4)

    def decode(w, pre, h, columns):
        rows = columns * TALL
        off = (HALO - h) * (TALL + 1)

        def body(n, _):
            base = pl.multiple_of(n * rows, 16)
            good = valid[pl.ds(base + off, rows), :] > 0
            near, far = operand(base, rows, TALL, (0, 2)), operand(base, rows, TALL, (2, 4))
            low = dot(near, stack(w.at[0]))
            high = dot(near, stack(w.at[1])) + dot(far, stack(w.at[0]))
            for t, (v, s) in enumerate(((low, 0), (low, 128), (high, 0), (high, 128))):
                v = v[:, s : s + 128]
                pre[t, pl.ds(base, rows), :] = v
                field[t, pl.ds(base, rows), :] = jnp.where(good, silu(v), 0.0)
            return 0

        lax.fori_loop(0, width(h) // columns, body, 0)

    decode(w1, pre1, 9, 17)
    spread(width(9), TALL, 4)
    decode(w2, pre2, 8, 16)

    def sum_columns(src, count, turn):
        rows = 6 * TALL

        def body(n, _):
            base = pl.multiple_of(n * rows, 8)
            total = None
            for l in range(3):
                v = src[pl.ds(base + l * TALL, rows), :]
                v = pltpu.roll(v, turn(l), 1) if turn(l) else v
                total = v if total is None else total + v
            mid[pl.ds(base, rows), :] = total
            return 0

        lax.fori_loop(0, -(-(count + 1) // 6), body, 0)

    def sum_rows(base, rows, turn):
        total = None
        for j in range(3):
            v = mid[pl.ds(base + j, rows), :]
            v = pltpu.roll(v, turn(j), 1) if turn(j) else v
            total = v if total is None else total + v
        return total

    def gather_taps(count, h, flip, stride):
        off = (HALO - h) * (TALL + 1)
        turn = lambda size: lambda n: (128 - size * (2 - n if flip else n)) % 128
        sum_columns(part, count, turn(12))
        lane = lax.broadcasted_iota(jnp.int32, (stride, 128), 1)

        def body(n, _):
            for c in range(6):
                x = jnp.minimum(n * 6 + c, count - 1)
                base = pl.multiple_of(x * TALL, 8)
                total = sum_rows(base, stride, turn(36))
                good = (valid[pl.ds(base + off, stride), :] > 0) & (lane < 12)
                pix[pl.ds(pl.multiple_of(x * stride, 8), stride), :] = jnp.where(good, total, 0.0)
            return 0

        lax.fori_loop(0, -(-count // 6), body, 0)

    def rgb_part(n, _):
        rows = 16 * TALL
        base = pl.multiple_of(n * rows, 16)
        a = jnp.concatenate([field[t, pl.ds(base, rows), :].astype(BF16) for t in range(4)], 1)
        part[pl.ds(base, rows), :] = dot_t(a, rgb_w[...])
        return 0

    lax.fori_loop(0, width(8) // 16, rgb_part, 0)
    gather_taps(width(7), 7, False, TALL)

    spread(width(7), TALL, 1, pix)

    def first(n, _):
        rows = 14 * TALL
        base = pl.multiple_of(n * rows, 16)
        good = valid[pl.ds(base + 4 * (TALL + 1), rows), :] > 0
        v = dot(operand(base, rows, TALL, (0, 1)), stack(one_taps))
        for t in range(2):
            p = v[:, t * 128 : t * 128 + 128]
            pref[t, pl.ds(base, rows), :] = p
            field[t, pl.ds(base, rows), :] = jnp.where(good, silu(p), 0.0)
        return 0

    lax.fori_loop(0, 2, first, 0)
    spread(width(6), TALL, 2)

    def second(n, _):
        rows = 13 * TALL
        base = pl.multiple_of(n * rows, 16)
        good = valid[pl.ds(base + 5 * (TALL + 1), rows), :] > 0
        low = dot(operand(base, rows, TALL, (0, 1)), stack(sec, slice(0, 128), slice(0, 256)))
        high = dot(operand(base, rows, TALL, (0, 2)), stack(sec, slice(None), slice(256, 512)))
        lane = lax.broadcasted_iota(jnp.int32, (rows, 128), 1)
        logits = jnp.zeros((rows, 128), F32)
        for t, (v, s) in enumerate(((low, 0), (low, 128), (high, 0), (high, 128))):
            v = v[:, s : s + 128]
            sg = sigmoid(v)
            score = jnp.sum(v * sg * head[...], axis=1, keepdims=True)
            push = -sigmoid(-score)
            logits = jnp.where(lane == t, score, logits)
            g = push * head[...] * (sg * (1.0 + v * (1.0 - sg)))
            field[t, pl.ds(base, rows), :] = jnp.where(good, g, 0.0)
        part[pl.ds(base, rows), :] = logits
        return 0

    lax.fori_loop(0, 2, second, 0)
    pick = jnp.where(
        lax.broadcasted_iota(jnp.int32, (16, 128), 0) == lax.broadcasted_iota(jnp.int32, (16, 128), 1), 1.0, 0.0
    ).astype(BF16)
    for x in range(COLS):
        v = dot_t(pick, part[pl.ds((x + 5) * TALL + 5, 128), :].astype(BF16))
        for t in range(4):
            line[t, x : x + 1, :] = v[t : t + 1]
    logit_ref[...] = line[:, :, 0:ROWS].astype(BF16)
    spread(width(5), TALL, 4)

    def second_back(n, _):
        rows = 12 * TALL
        base = pl.multiple_of(n * rows, 16)
        good = valid[pl.ds(base + 6 * (TALL + 1), rows), :] > 0
        v = dot_t(operand(base, rows, TALL, (0, 4)), across(sec))
        g = []
        for t in range(2):
            p = pref[t, pl.ds(base + 2 * (TALL + 1), rows), :]
            g.append(jnp.where(good, v[:, t * 128 : t * 128 + 128] * dsilu(p), 0.0).astype(BF16))
        part[pl.ds(base, rows), :] = dot_t(jnp.concatenate(g, 1), one_w[...])
        return 0

    lax.fori_loop(0, 2, second_back, 0)
    gather_taps(width(3), 3, True, SHORT)

    spread(width(3), SHORT, 1, pix)
    flipped = jnp.concatenate([rgb_taps[8 - n] for n in range(9)], 0)
    back = dot(operand(0, width(2) * SHORT, SHORT, (0, 1)), flipped)
    for t in range(4):
        for x in range(width(2)):
            p = pre2[t, pl.ds((x + 6) * TALL + 6, SHORT), :]
            g = back[x * SHORT : (x + 1) * SHORT, t * 128 : t * 128 + 128] * dsilu(p)
            good = valid_s[pl.ds(x * SHORT, SHORT), :] > 0
            field[t, pl.ds(x * SHORT, SHORT), :] = jnp.where(good, g, 0.0)
    spread(width(2), SHORT, 4)

    def back_conv(w, count):
        rows = count * SHORT
        near, far = operand(0, rows, SHORT, (0, 2)), operand(0, rows, SHORT, (2, 4))
        high = dot_t(far, across(w.at[0]))
        low = dot_t(far, across(w.at[1])) + dot_t(near, across(w.at[0]))
        return [v[:, s : s + 128] for v in (low, high) for s in (0, 128)]

    back = back_conv(w2, width(1))
    for t in range(4):
        for x in range(width(1)):
            p = pre1[t, pl.ds((x + 8) * TALL + 8, SHORT), :]
            g = back[t][x * SHORT : (x + 1) * SHORT] * dsilu(p)
            good = valid_s[pl.ds((x + 1) * SHORT + 1, SHORT), :] > 0
            field[t, pl.ds(x * SHORT, SHORT), :] = jnp.where(good, g, 0.0)
    spread(width(1), SHORT, 4)
    back = back_conv(w1, width(0))
    for t in range(4):
        field[t, 0 : COLS * SHORT, :] = back[t]
    for t in range(4):
        for y in range(ROWS):
            out_ref[t, y] = field[t, pl.ds(y, COLS, SHORT), :].astype(BF16)


def per_device(latent, conv_one, conv_two, to_rgb, disc_one, disc_two, disc_head):
    x = latent[0]

    vmem = pl.BlockSpec(memory_space=pltpu.VMEM)
    hbm = pl.BlockSpec(memory_space=pl.ANY)

    def exchange(first, last, axis):
        n = lax.axis_size(axis)
        before = lax.ppermute(last, axis, [(i, (i + 1) % n) for i in range(n)])
        after = lax.ppermute(first, axis, [((i + 1) % n, i) for i in range(n)])
        return before, after

    first, last = pl.pallas_call(
        cut_columns,
        out_shape=[jax.ShapeDtypeStruct((HALO, 4, ROWS, 128), BF16)] * 2,
        in_specs=[vmem],
        out_specs=[vmem] * 2,
        scratch_shapes=[pltpu.VMEM((4, ROWS * COLS, 128), F32)],
        compiler_params=pltpu.CompilerParams(vmem_limit_bytes=8 << 20),
    )(x)
    left, right = exchange(first, last, "gx")
    first, last = pl.pallas_call(
        cut_rows,
        out_shape=[jax.ShapeDtypeStruct((4, WIDE * HALO, 128), BF16)] * 2,
        in_specs=[vmem] * 3,
        out_specs=[vmem] * 2,
        scratch_shapes=[pltpu.VMEM((2, 4, WIDE * HALO, 128), F32)],
        compiler_params=pltpu.CompilerParams(vmem_limit_bytes=8 << 20),
    )(x, left, right)
    top, bottom = exchange(first, last, "gy")
    taps = lambda k: k.reshape(3, 9, *k.shape[3:])
    rgb_rows = jnp.swapaxes(to_rgb, 3, 4).reshape(81, 128).astype(F32)
    one_rows = jnp.pad(disc_one.reshape(81, 64).astype(F32), ((0, 0), (0, 64)))
    p = WIDE * TALL + PAD
    shapes = [(2, 9, 256, 256), (2, 9, 256, 256), (9, 256, 512), (128, 512), (128, 256), (9, 128, 512), (9, 128, 256)]
    weights = pl.pallas_call(
        lay_out,
        out_shape=[jax.ShapeDtypeStruct(n, BF16) for n in shapes],
        in_specs=[hbm, hbm, hbm, vmem, vmem],
        out_specs=[vmem] * 7,
        scratch_shapes=[pltpu.VMEM((128, 512), F32), pltpu.SemaphoreType.DMA((24,))],
        compiler_params=pltpu.CompilerParams(vmem_limit_bytes=16 << 20),
        cost_estimate=pl.CostEstimate(flops=0, bytes_accessed=12 << 20, transcendentals=0),
    )(taps(conv_one), taps(conv_two), taps(disc_two), rgb_rows, one_rows)
    out, logits = pl.pallas_call(
        kernel,
        out_shape=[
            jax.ShapeDtypeStruct((4, ROWS, COLS, 128), BF16),
            jax.ShapeDtypeStruct((4, COLS, ROWS), BF16),
        ],
        in_specs=[vmem] * 13,
        out_specs=[vmem, vmem],
        scratch_shapes=[
            pltpu.VMEM((4, p, 128), F32),
            pltpu.VMEM((4, p, 128), F32),
            pltpu.VMEM((4, p, 128), F32),
            pltpu.VMEM((2, p, 128), F32),
            pltpu.VMEM((3, p, 512), BF16),
            pltpu.VMEM((p, 128), F32),
            pltpu.VMEM((p, 128), F32),
            pltpu.VMEM((p, 128), F32),
            pltpu.VMEM((p, 128), F32),
            pltpu.VMEM((p, 128), F32),
            pltpu.VMEM((4, COLS, 128), F32),
            pltpu.VMEM((2, 4, WIDE * HALO, 128), F32),
        ],
        compiler_params=pltpu.CompilerParams(vmem_limit_bytes=34 << 20),
    )(x, left, right, top, bottom, *weights, disc_head.reshape(1, 128))
    return out[None], jnp.swapaxes(logits, 1, 2)[None]


def solution(mesh):
    placed = (P(None, None, "gy", "gx", None), P(), P(), P(), P(), P(), P())
    return jax.shard_map(
        per_device,
        mesh=mesh,
        in_specs=placed,
        out_specs=(P(None, None, "gy", "gx", None), P(None, None, "gy", "gx")),
        check_vma=False,
    )
```

```python
import jax
import jax.numpy as jnp
import numpy as np
from jax import lax
from jax.experimental import pallas as pl
from jax.experimental.pallas import tpu as pltpu
from jax.sharding import PartitionSpec as P

F32 = jnp.float32
BF16 = jnp.bfloat16

HALO = 10
ROWS, COLS = 24, 16
TALL = 48
SHORT = 32
WIDE = COLS + 2 * HALO
HIGH = ROWS + 2 * HALO
PAD = 256


def width(h):
    return COLS + 2 * h


def sigmoid(v):
    return 0.5 * jnp.tanh(0.5 * v) + 0.5


def silu(v):
    half = 0.5 * v
    return half + half * jnp.tanh(half)


def dsilu(v):
    s = sigmoid(v)
    return s * (1.0 + v * (1.0 - s))


def lay_out(k1, k2, ks, rgb_rows, one_rows, wide, sec, rgb_w, one_w, rgb_taps, one_taps, small, sems):
    loads = []
    for k, w in ((k1, wide.at[0]), (k2, wide.at[1])):
        for far in range(2):
            for f in range(2):
                for t in range(2):
                    i = f - t + 2 - 2 * far
                    block = w.at[far, :, f * 128 : f * 128 + 128, t * 128 : t * 128 + 128]
                    if 0 <= i <= 2:
                        loads.append(pltpu.make_async_copy(k.at[i], block, sems.at[len(loads)]))
                    else:
                        block[...] = jnp.zeros(block.shape, BF16)
    for f in range(4):
        for t in range(4):
            i = f - t + 2
            block = sec.at[:, f * 64 : f * 64 + 64, t * 128 : t * 128 + 128]
            if 0 <= i <= 2:
                loads.append(pltpu.make_async_copy(ks.at[i], block, sems.at[len(loads)]))
            else:
                block[...] = jnp.zeros(block.shape, BF16)
    for c in loads:
        c.start()

    mine = lax.broadcasted_iota(jnp.int32, (16, 1), 0) < 12
    for rows, out, each, lanes, first in (
        (rgb_rows, rgb_w, rgb_taps, 128, True),
        (one_rows, one_w, one_taps, 64, False),
    ):
        small[...] = jnp.zeros_like(small)
        for f in range(4):
            for t in range(4):
                i = (t - f if first else f - t) + 2
                if 0 <= i <= 2:
                    for n in range(9):
                        small[n * 12 + f * 3 : n * 12 + f * 3 + 3, t * lanes : t * lanes + lanes] = rows[
                            (i * 9 + n) * 3 : (i * 9 + n) * 3 + 3, 0:lanes
                        ]
        out[...] = small[:, 0 : 4 * lanes].astype(BF16)
        each[...] = jnp.zeros_like(each)
        for n in range(9):
            v = small[n * 12 : n * 12 + 16, 0 : 4 * lanes]
            each[n, 0:16] = jnp.where(mine, v, 0.0).astype(BF16)
    for c in loads:
        c.wait()


def cut_columns(own, first, last, rows):
    for t in range(4):
        rows[t] = own[t].reshape(ROWS * COLS, 128).astype(F32)
    for x in range(HALO):
        for t in range(4):
            first[x, t] = rows[t, pl.ds(x, ROWS, COLS), :].astype(BF16)
            last[x, t] = rows[t, pl.ds(COLS - HALO + x, ROWS, COLS), :].astype(BF16)


def cut_rows(own, left, right, first, last, rows):
    low = ROWS - HALO
    gx, nx = lax.axis_index("gx"), lax.axis_size("gx")
    inside = (jnp.where(gx > 0, 1.0, 0.0).astype(F32), jnp.where(gx < nx - 1, 1.0, 0.0).astype(F32))
    for t in range(4):
        for y in range(HALO):
            rows[0, t, pl.ds(HALO * HALO + y, COLS, HALO), :] = own[t, y].astype(F32)
            rows[1, t, pl.ds(HALO * HALO + y, COLS, HALO), :] = own[t, low + y].astype(F32)
        for ref, start, good in ((left, 0, inside[0]), (right, HALO + COLS, inside[1])):
            for x in range(HALO):
                v = ref[x, t].astype(F32) * good
                at = (start + x) * HALO
                rows[0, t, at : at + HALO, :] = v[0:HALO]
                rows[1, t, at : at + HALO, :] = v[low:ROWS]
        first[t] = rows[0, t].astype(BF16)
        last[t] = rows[1, t].astype(BF16)


def kernel(
    own, left, right, top, bottom, wide, sec, rgb_w, one_w, rgb_taps, one_taps, head,
    out_ref, logit_ref,
    field, pre, res, pref, taps, valid, valid_s, part, pix, mid, line, edge,
):
    gy, gx = lax.axis_index("gy"), lax.axis_index("gx")
    ny, nx = lax.axis_size("gy"), lax.axis_size("gx")

    def validity(ref, stride, h):
        first_x, first_y = gx * COLS - h, gy * ROWS - h
        y = first_y + lax.broadcasted_iota(jnp.int32, (stride, 128), 0)
        good_y = jnp.where((y >= 0) & (y < ny * ROWS), 1.0, 0.0).astype(F32)

        def body(x, _):
            place = first_x + x
            good_x = jnp.where((place >= 0) & (place < nx * COLS), 1.0, 0.0).astype(F32)
            ref[pl.ds(pl.multiple_of(x * stride, 8), stride), :] = good_y * good_x
            return 0

        lax.fori_loop(0, width(h), body, 0)

    validity(valid, TALL, HALO)
    validity(valid_s, SHORT, 2)

    def spread(count, stride, tiles, source=None):
        step = 96

        def body(n, _):
            r = pl.multiple_of(n * step, 32)
            for j in range(3):
                for t in range(tiles):
                    v = field[t, pl.ds(r + j, step), :] if source is None else source[pl.ds(r + j, step), :]
                    taps[j, pl.ds(r, step), t * 128 : t * 128 + 128] = v.astype(BF16)
            return 0

        lax.fori_loop(0, -(-count * stride // step), body, 0)

    def operand(base, rows, stride, tiles):
        return jnp.concatenate(
            [
                taps[j, pl.ds(pl.multiple_of(base + l * stride, 16), rows), tiles[0] * 128 : tiles[1] * 128]
                for j in range(3)
                for l in range(3)
            ],
            1,
        )

    def stack(w, rows=slice(None), lanes=slice(None)):
        v = w[:, rows, lanes]
        return v.reshape(-1, v.shape[-1])

    def across(w):
        return jnp.concatenate([w[8 - n] for n in range(9)], 1)

    def dot_t(a, b):
        return lax.dot_general(a, b, (((1,), (1,)), ((), ())), preferred_element_type=F32)

    def dot(a, b):
        return jnp.dot(a, b, preferred_element_type=F32)

    def place(n, _):
        for t in range(4):
            field[t, pl.ds(HALO * TALL + HALO + n, COLS, TALL), :] = own[t, n].astype(F32)
        return 0

    lax.fori_loop(0, ROWS, place, 0, unroll=4)
    one = lambda test: jnp.where(test, 1.0, 0.0).astype(F32)
    for t in range(4):
        for x in range(HALO):
            for ref, start, good in ((left, 0, one(gx > 0)), (right, HALO + COLS, one(gx < nx - 1))):
                at = (start + x) * TALL + HALO
                field[t, at : at + ROWS, :] = ref[x, t].astype(F32) * good
        for n, (ref, y, good) in enumerate(((top, 0, one(gy > 0)), (bottom, HALO + ROWS, one(gy < ny - 1)))):
            edge[n, t] = ref[t].astype(F32) * good
            for x in range(WIDE):
                field[t, x * TALL + y : x * TALL + y + HALO, :] = edge[n, t, x * HALO : x * HALO + HALO, :]
    spread(WIDE, TALL, 4)

    def decode(k, _):
        rows = 17 * TALL
        off = (k + 1) * (TALL + 1)

        def body(n, _):
            base = pl.multiple_of(n * rows, 16)
            good = valid[pl.ds(base + off, rows), :] > 0
            near, far = operand(base, rows, TALL, (0, 2)), operand(base, rows, TALL, (2, 4))
            low = dot(near, stack(wide.at[k, 0]))
            high = dot(near, stack(wide.at[k, 1])) + dot(far, stack(wide.at[k, 0]))
            for t, (v, s) in enumerate(((low, 0), (low, 128), (high, 0), (high, 128))):
                v = v[:, s : s + 128]
                pre[k, t, pl.ds(base, rows), :] = v
                field[t, pl.ds(base, rows), :] = jnp.where(good, silu(v), 0.0)
            return 0

        lax.fori_loop(0, 2, body, 0)

        @pl.when(k == 0)
        def _():
            spread(width(9), TALL, 4)

        return 0

    lax.fori_loop(0, 2, decode, 0)

    def sum_columns(src, count, turn):
        rows = 6 * TALL

        def body(n, _):
            base = pl.multiple_of(n * rows, 8)
            total = None
            for l in range(3):
                v = src[pl.ds(base + l * TALL, rows), :]
                v = pltpu.roll(v, turn(l), 1) if turn(l) else v
                total = v if total is None else total + v
            mid[pl.ds(base, rows), :] = total
            return 0

        lax.fori_loop(0, -(-(count + 1) // 6), body, 0)

    def sum_rows(base, rows, turn):
        total = None
        for j in range(3):
            v = mid[pl.ds(base + j, rows), :]
            v = pltpu.roll(v, turn(j), 1) if turn(j) else v
            total = v if total is None else total + v
        return total

    def gather_taps(count, h, flip, stride):
        off = (HALO - h) * (TALL + 1)
        turn = lambda size: lambda n: (128 - size * (2 - n if flip else n)) % 128
        sum_columns(part, count, turn(12))
        lane = lax.broadcasted_iota(jnp.int32, (stride, 128), 1)

        def body(n, _):
            for c in range(6):
                x = jnp.minimum(n * 6 + c, count - 1)
                base = pl.multiple_of(x * TALL, 8)
                total = sum_rows(base, stride, turn(36))
                good = (valid[pl.ds(base + off, stride), :] > 0) & (lane < 12)
                pix[pl.ds(pl.multiple_of(x * stride, 8), stride), :] = jnp.where(good, total, 0.0)
            return 0

        lax.fori_loop(0, -(-count // 6), body, 0)

    def rgb_part(n, _):
        rows = 16 * TALL
        base = pl.multiple_of(n * rows, 16)
        a = jnp.concatenate([field[t, pl.ds(base, rows), :].astype(BF16) for t in range(4)], 1)
        part[pl.ds(base, rows), :] = dot_t(a, rgb_w[...])
        return 0

    lax.fori_loop(0, width(8) // 16, rgb_part, 0)
    gather_taps(width(7), 7, False, TALL)

    spread(width(7), TALL, 1, pix)

    def first(n, _):
        rows = 14 * TALL
        base = pl.multiple_of(n * rows, 16)
        good = valid[pl.ds(base + 4 * (TALL + 1), rows), :] > 0
        v = dot(operand(base, rows, TALL, (0, 1)), stack(one_taps))
        for t in range(2):
            p = v[:, t * 128 : t * 128 + 128]
            pref[t, pl.ds(base, rows), :] = p
            field[t, pl.ds(base, rows), :] = jnp.where(good, silu(p), 0.0)
        return 0

    lax.fori_loop(0, 2, first, 0)
    spread(width(6), TALL, 2)

    def second(n, _):
        rows = 13 * TALL
        base = pl.multiple_of(n * rows, 16)
        good = valid[pl.ds(base + 5 * (TALL + 1), rows), :] > 0
        low = dot(operand(base, rows, TALL, (0, 1)), stack(sec, slice(0, 128), slice(0, 256)))
        high = dot(operand(base, rows, TALL, (0, 2)), stack(sec, slice(None), slice(256, 512)))
        lane = lax.broadcasted_iota(jnp.int32, (rows, 128), 1)
        logits = jnp.zeros((rows, 128), F32)
        for t, (v, s) in enumerate(((low, 0), (low, 128), (high, 0), (high, 128))):
            v = v[:, s : s + 128]
            sg = sigmoid(v)
            score = jnp.sum(v * sg * head[...], axis=1, keepdims=True)
            push = -sigmoid(-score)
            logits = jnp.where(lane == t, score, logits)
            g = push * head[...] * (sg * (1.0 + v * (1.0 - sg)))
            field[t, pl.ds(base, rows), :] = jnp.where(good, g, 0.0)
        part[pl.ds(base, rows), :] = logits
        return 0

    lax.fori_loop(0, 2, second, 0)
    pick = jnp.where(
        lax.broadcasted_iota(jnp.int32, (16, 128), 0) == lax.broadcasted_iota(jnp.int32, (16, 128), 1), 1.0, 0.0
    ).astype(BF16)
    for x in range(COLS):
        v = dot_t(pick, part[pl.ds((x + 5) * TALL + 5, 128), :].astype(BF16))
        for t in range(4):
            line[t, x : x + 1, :] = v[t : t + 1]
    logit_ref[...] = line[:, :, 0:ROWS].astype(BF16)
    spread(width(5), TALL, 4)

    def second_back(n, _):
        rows = 12 * TALL
        base = pl.multiple_of(n * rows, 16)
        good = valid[pl.ds(base + 6 * (TALL + 1), rows), :] > 0
        v = dot_t(operand(base, rows, TALL, (0, 4)), across(sec))
        g = []
        for t in range(2):
            p = pref[t, pl.ds(base + 2 * (TALL + 1), rows), :]
            g.append(jnp.where(good, v[:, t * 128 : t * 128 + 128] * dsilu(p), 0.0).astype(BF16))
        part[pl.ds(base, rows), :] = dot_t(jnp.concatenate(g, 1), one_w[...])
        return 0

    lax.fori_loop(0, 2, second_back, 0)
    gather_taps(width(3), 3, True, SHORT)

    spread(width(3), SHORT, 1, pix)
    flipped = jnp.concatenate([rgb_taps[8 - n] for n in range(9)], 0)
    back = dot(operand(0, width(2) * SHORT, SHORT, (0, 1)), flipped)
    for t in range(4):
        res[t] = back[:, t * 128 : t * 128 + 128]

    def temper(k, h):
        away = 9 - k - h

        def body(x, _):
            base = pl.multiple_of(x * SHORT, 8)
            good = valid_s[pl.ds((x + 2 - h) * SHORT + 2 - h, SHORT), :] > 0
            for t in range(4):
                p = pre[k, t, pl.ds((x + away) * TALL + away, SHORT), :]
                g = res[t, pl.ds(base, SHORT), :] * dsilu(p)
                field[t, pl.ds(base, SHORT), :] = jnp.where(good, g, 0.0)
            return 0

        lax.fori_loop(0, width(h), body, 0, unroll=2)

    temper(1, 2)

    def back_conv(n, _):
        rows = width(1) * SHORT
        spread(width(2), SHORT, 4)
        k = 1 - n
        near, far = operand(0, rows, SHORT, (0, 2)), operand(0, rows, SHORT, (2, 4))
        high = dot_t(far, across(wide.at[k, 0]))
        low = dot_t(far, across(wide.at[k, 1])) + dot_t(near, across(wide.at[k, 0]))
        for t, (v, s) in enumerate(((low, 0), (low, 128), (high, 0), (high, 128))):
            res[t, 0:rows, :] = v[:, s : s + 128]

        @pl.when(n == 0)
        def _():
            temper(0, 1)

        return 0

    lax.fori_loop(0, 2, back_conv, 0)

    def emit(y, _):
        for t in range(4):
            out_ref[t, y] = res[t, pl.ds(y, COLS, SHORT), :].astype(BF16)
        return 0

    lax.fori_loop(0, ROWS, emit, 0, unroll=4)


def per_device(latent, conv_one, conv_two, to_rgb, disc_one, disc_two, disc_head):
    x = latent[0]

    vmem = pl.BlockSpec(memory_space=pltpu.VMEM)
    hbm = pl.BlockSpec(memory_space=pl.ANY)

    def exchange(first, last, axis):
        n = lax.axis_size(axis)
        before = lax.ppermute(last, axis, [(i, (i + 1) % n) for i in range(n)])
        after = lax.ppermute(first, axis, [((i + 1) % n, i) for i in range(n)])
        return before, after

    first, last = pl.pallas_call(
        cut_columns,
        out_shape=[jax.ShapeDtypeStruct((HALO, 4, ROWS, 128), BF16)] * 2,
        in_specs=[vmem],
        out_specs=[vmem] * 2,
        scratch_shapes=[pltpu.VMEM((4, ROWS * COLS, 128), F32)],
        compiler_params=pltpu.CompilerParams(vmem_limit_bytes=8 << 20),
    )(x)
    left, right = exchange(first, last, "gx")
    first, last = pl.pallas_call(
        cut_rows,
        out_shape=[jax.ShapeDtypeStruct((4, WIDE * HALO, 128), BF16)] * 2,
        in_specs=[vmem] * 3,
        out_specs=[vmem] * 2,
        scratch_shapes=[pltpu.VMEM((2, 4, WIDE * HALO, 128), F32)],
        compiler_params=pltpu.CompilerParams(vmem_limit_bytes=8 << 20),
    )(x, left, right)
    top, bottom = exchange(first, last, "gy")
    taps = lambda k: k.reshape(3, 9, *k.shape[3:])
    rgb_rows = jnp.swapaxes(to_rgb, 3, 4).reshape(81, 128).astype(F32)
    one_rows = jnp.pad(disc_one.reshape(81, 64).astype(F32), ((0, 0), (0, 64)))
    p = WIDE * TALL + PAD
    shapes = [(2, 2, 9, 256, 256), (9, 256, 512), (128, 512), (128, 256), (9, 128, 512), (9, 128, 256)]
    weights = pl.pallas_call(
        lay_out,
        out_shape=[jax.ShapeDtypeStruct(n, BF16) for n in shapes],
        in_specs=[hbm, hbm, hbm, vmem, vmem],
        out_specs=[vmem] * 6,
        scratch_shapes=[pltpu.VMEM((128, 512), F32), pltpu.SemaphoreType.DMA((24,))],
        compiler_params=pltpu.CompilerParams(vmem_limit_bytes=16 << 20),
        cost_estimate=pl.CostEstimate(flops=0, bytes_accessed=12 << 20, transcendentals=0),
    )(taps(conv_one), taps(conv_two), taps(disc_two), rgb_rows, one_rows)
    out, logits = pl.pallas_call(
        kernel,
        out_shape=[
            jax.ShapeDtypeStruct((4, ROWS, COLS, 128), BF16),
            jax.ShapeDtypeStruct((4, COLS, ROWS), BF16),
        ],
        in_specs=[vmem] * 12,
        out_specs=[vmem, vmem],
        scratch_shapes=[
            pltpu.VMEM((4, p, 128), F32),
            pltpu.VMEM((2, 4, p, 128), F32),
            pltpu.VMEM((4, (COLS + 4) * SHORT, 128), F32),
            pltpu.VMEM((2, p, 128), F32),
            pltpu.VMEM((3, p, 512), BF16),
            pltpu.VMEM((p, 128), F32),
            pltpu.VMEM((p, 128), F32),
            pltpu.VMEM((p, 128), F32),
            pltpu.VMEM((p, 128), F32),
            pltpu.VMEM((p, 128), F32),
            pltpu.VMEM((4, COLS, 128), F32),
            pltpu.VMEM((2, 4, WIDE * HALO, 128), F32),
        ],
        compiler_params=pltpu.CompilerParams(vmem_limit_bytes=36 << 20),
    )(x, left, right, top, bottom, *weights, disc_head.reshape(1, 128))
    return out[None], jnp.swapaxes(logits, 1, 2)[None]


def solution(mesh):
    placed = (P(None, None, "gy", "gx", None), P(), P(), P(), P(), P(), P())
    return jax.shard_map(
        per_device,
        mesh=mesh,
        in_specs=placed,
        out_specs=(P(None, None, "gy", "gx", None), P(None, None, "gy", "gx")),
        check_vma=False,
    )
```

```python
import jax
import jax.numpy as jnp
import numpy as np
from jax import lax
from jax.experimental import pallas as pl
from jax.experimental.pallas import tpu as pltpu
from jax.sharding import PartitionSpec as P

F32 = jnp.float32
BF16 = jnp.bfloat16

HALO = 10
ROWS, COLS = 24, 16
TALL = 48
SHORT = 32
WIDE = COLS + 2 * HALO
HIGH = ROWS + 2 * HALO
PAD = 256


def width(h):
    return COLS + 2 * h


def sigmoid(v):
    return 0.5 * jnp.tanh(0.5 * v) + 0.5


def silu(v):
    half = 0.5 * v
    return half + half * jnp.tanh(half)


def dsilu(v):
    s = sigmoid(v)
    return s * (1.0 + v * (1.0 - s))


def lay_out(k1, k2, ks, rgb_rows, one_rows, wide, sec, rgb_w, one_w, rgb_taps, one_taps, valid, valid_s, small, sems):
    loads = []
    for k, w in ((k1, wide.at[0]), (k2, wide.at[1])):
        for far in range(2):
            for f in range(2):
                for t in range(2):
                    i = f - t + 2 - 2 * far
                    block = w.at[far, :, f * 128 : f * 128 + 128, t * 128 : t * 128 + 128]
                    if 0 <= i <= 2:
                        loads.append(pltpu.make_async_copy(k.at[i], block, sems.at[len(loads)]))
                    else:
                        block[...] = jnp.zeros(block.shape, BF16)
    for f in range(4):
        for t in range(4):
            i = f - t + 2
            block = sec.at[:, f * 64 : f * 64 + 64, t * 128 : t * 128 + 128]
            if 0 <= i <= 2:
                loads.append(pltpu.make_async_copy(ks.at[i], block, sems.at[len(loads)]))
            else:
                block[...] = jnp.zeros(block.shape, BF16)
    for c in loads:
        c.start()

    gy, gx = lax.axis_index("gy"), lax.axis_index("gx")
    ny, nx = lax.axis_size("gy"), lax.axis_size("gx")

    def validity(ref, stride, h):
        first_x, first_y = gx * COLS - h, gy * ROWS - h
        y = first_y + lax.broadcasted_iota(jnp.int32, (stride, 128), 0)
        good_y = jnp.where((y >= 0) & (y < ny * ROWS), 1.0, 0.0).astype(F32)

        def body(x, _):
            place = first_x + x
            good_x = jnp.where((place >= 0) & (place < nx * COLS), 1.0, 0.0).astype(F32)
            ref[pl.ds(pl.multiple_of(x * stride, 8), stride), :] = good_y * good_x
            return 0

        lax.fori_loop(0, width(h), body, 0)

    validity(valid, TALL, HALO)
    validity(valid_s, SHORT, 2)

    mine = lax.broadcasted_iota(jnp.int32, (16, 1), 0) < 12
    for rows, out, each, lanes, first in (
        (rgb_rows, rgb_w, rgb_taps, 128, True),
        (one_rows, one_w, one_taps, 64, False),
    ):
        small[...] = jnp.zeros_like(small)
        for f in range(4):
            for t in range(4):
                i = (t - f if first else f - t) + 2
                if 0 <= i <= 2:
                    for n in range(9):
                        small[n * 12 + f * 3 : n * 12 + f * 3 + 3, t * lanes : t * lanes + lanes] = rows[
                            (i * 9 + n) * 3 : (i * 9 + n) * 3 + 3, 0:lanes
                        ]
        out[...] = small[:, 0 : 4 * lanes].astype(BF16)
        each[...] = jnp.zeros_like(each)
        for n in range(9):
            v = small[n * 12 : n * 12 + 16, 0 : 4 * lanes]
            each[n, 0:16] = jnp.where(mine, v, 0.0).astype(BF16)
    for c in loads:
        c.wait()


def cut_columns(own, first, last, rows):
    for t in range(4):
        rows[t] = own[t].reshape(ROWS * COLS, 128).astype(F32)
    for x in range(HALO):
        for t in range(4):
            first[x, t] = rows[t, pl.ds(x, ROWS, COLS), :].astype(BF16)
            last[x, t] = rows[t, pl.ds(COLS - HALO + x, ROWS, COLS), :].astype(BF16)


def cut_rows(own, left, right, first, last, rows):
    low = ROWS - HALO
    gx, nx = lax.axis_index("gx"), lax.axis_size("gx")
    inside = (jnp.where(gx > 0, 1.0, 0.0).astype(F32), jnp.where(gx < nx - 1, 1.0, 0.0).astype(F32))
    for t in range(4):
        for y in range(HALO):
            rows[0, t, pl.ds(HALO * HALO + y, COLS, HALO), :] = own[t, y].astype(F32)
            rows[1, t, pl.ds(HALO * HALO + y, COLS, HALO), :] = own[t, low + y].astype(F32)
        for ref, start, good in ((left, 0, inside[0]), (right, HALO + COLS, inside[1])):
            for x in range(HALO):
                v = ref[x, t].astype(F32) * good
                at = (start + x) * HALO
                rows[0, t, at : at + HALO, :] = v[0:HALO]
                rows[1, t, at : at + HALO, :] = v[low:ROWS]
        first[t] = rows[0, t].astype(BF16)
        last[t] = rows[1, t].astype(BF16)


def kernel(
    own, left, right, top, bottom, wide, sec, rgb_w, one_w, rgb_taps, one_taps, valid, valid_s, head,
    out_ref, logit_ref,
    field, pre, res, pref, taps, part, pix, mid, line, edge,
):
    gy, gx = lax.axis_index("gy"), lax.axis_index("gx")
    ny, nx = lax.axis_size("gy"), lax.axis_size("gx")

    def spread(count, stride, tiles, source=None):
        step = 96

        def body(n, _):
            r = pl.multiple_of(n * step, 32)
            for j in range(3):
                for t in range(tiles):
                    v = field[t, pl.ds(r + j, step), :] if source is None else source[pl.ds(r + j, step), :]
                    taps[j, pl.ds(r, step), t * 128 : t * 128 + 128] = v.astype(BF16)
            return 0

        lax.fori_loop(0, -(-count * stride // step), body, 0)

    def operand(base, rows, stride, tiles):
        return jnp.concatenate(
            [
                taps[j, pl.ds(pl.multiple_of(base + l * stride, 16), rows), tiles[0] * 128 : tiles[1] * 128]
                for j in range(3)
                for l in range(3)
            ],
            1,
        )

    def stack(w, rows=slice(None), lanes=slice(None)):
        v = w[:, rows, lanes]
        return v.reshape(-1, v.shape[-1])

    def across(w):
        return jnp.concatenate([w[8 - n] for n in range(9)], 1)

    def dot_t(a, b):
        return lax.dot_general(a, b, (((1,), (1,)), ((), ())), preferred_element_type=F32)

    def dot(a, b):
        return jnp.dot(a, b, preferred_element_type=F32)

    def place(n, _):
        for t in range(4):
            field[t, pl.ds(HALO * TALL + HALO + n, COLS, TALL), :] = own[t, n].astype(F32)
        return 0

    lax.fori_loop(0, ROWS, place, 0, unroll=4)
    one = lambda test: jnp.where(test, 1.0, 0.0).astype(F32)
    for t in range(4):
        for x in range(HALO):
            for ref, start, good in ((left, 0, one(gx > 0)), (right, HALO + COLS, one(gx < nx - 1))):
                at = (start + x) * TALL + HALO
                field[t, at : at + ROWS, :] = ref[x, t].astype(F32) * good
        for n, (ref, y, good) in enumerate(((top, 0, one(gy > 0)), (bottom, HALO + ROWS, one(gy < ny - 1)))):
            edge[n, t] = ref[t].astype(F32) * good
            for x in range(WIDE):
                field[t, x * TALL + y : x * TALL + y + HALO, :] = edge[n, t, x * HALO : x * HALO + HALO, :]
    spread(WIDE, TALL, 4)

    def decode(k, _):
        rows = 17 * TALL
        off = (k + 1) * (TALL + 1)

        def body(n, _):
            base = pl.multiple_of(n * rows, 16)
            good = valid[pl.ds(base + off, rows), :] > 0
            near, far = operand(base, rows, TALL, (0, 2)), operand(base, rows, TALL, (2, 4))
            low = dot(near, stack(wide.at[k, 0]))
            high = dot(near, stack(wide.at[k, 1])) + dot(far, stack(wide.at[k, 0]))
            for t, (v, s) in enumerate(((low, 0), (low, 128), (high, 0), (high, 128))):
                v = v[:, s : s + 128]
                pre[k, t, pl.ds(base, rows), :] = v
                field[t, pl.ds(base, rows), :] = jnp.where(good, silu(v), 0.0)
            return 0

        lax.fori_loop(0, 2, body, 0)

        @pl.when(k == 0)
        def _():
            spread(width(9), TALL, 4)

        return 0

    lax.fori_loop(0, 2, decode, 0)

    def sum_columns(src, count, turn):
        rows = 6 * TALL

        def body(n, _):
            base = pl.multiple_of(n * rows, 8)
            total = None
            for l in range(3):
                v = src[pl.ds(base + l * TALL, rows), :]
                v = pltpu.roll(v, turn(l), 1) if turn(l) else v
                total = v if total is None else total + v
            mid[pl.ds(base, rows), :] = total
            return 0

        lax.fori_loop(0, -(-(count + 1) // 6), body, 0)

    def sum_rows(base, rows, turn):
        total = None
        for j in range(3):
            v = mid[pl.ds(base + j, rows), :]
            v = pltpu.roll(v, turn(j), 1) if turn(j) else v
            total = v if total is None else total + v
        return total

    def gather_taps(count, h, flip, stride):
        off = (HALO - h) * (TALL + 1)
        turn = lambda size: lambda n: (128 - size * (2 - n if flip else n)) % 128
        sum_columns(part, count, turn(12))
        lane = lax.broadcasted_iota(jnp.int32, (stride, 128), 1)

        def body(n, _):
            for c in range(6):
                x = jnp.minimum(n * 6 + c, count - 1)
                base = pl.multiple_of(x * TALL, 8)
                total = sum_rows(base, stride, turn(36))
                good = (valid[pl.ds(base + off, stride), :] > 0) & (lane < 12)
                pix[pl.ds(pl.multiple_of(x * stride, 8), stride), :] = jnp.where(good, total, 0.0)
            return 0

        lax.fori_loop(0, -(-count // 6), body, 0)

    def rgb_part(n, _):
        rows = 16 * TALL
        base = pl.multiple_of(n * rows, 16)
        a = jnp.concatenate([field[t, pl.ds(base, rows), :].astype(BF16) for t in range(4)], 1)
        part[pl.ds(base, rows), :] = dot_t(a, rgb_w[...])
        return 0

    lax.fori_loop(0, width(8) // 16, rgb_part, 0)
    gather_taps(width(7), 7, False, TALL)

    spread(width(7), TALL, 1, pix)

    def first(n, _):
        rows = 14 * TALL
        base = pl.multiple_of(n * rows, 16)
        good = valid[pl.ds(base + 4 * (TALL + 1), rows), :] > 0
        v = dot(operand(base, rows, TALL, (0, 1)), stack(one_taps))
        for t in range(2):
            p = v[:, t * 128 : t * 128 + 128]
            pref[t, pl.ds(base, rows), :] = p
            field[t, pl.ds(base, rows), :] = jnp.where(good, silu(p), 0.0)
        return 0

    lax.fori_loop(0, 2, first, 0)
    spread(width(6), TALL, 2)

    def second(n, _):
        rows = 13 * TALL
        base = pl.multiple_of(n * rows, 16)
        good = valid[pl.ds(base + 5 * (TALL + 1), rows), :] > 0
        low = dot(operand(base, rows, TALL, (0, 1)), stack(sec, slice(0, 128), slice(0, 256)))
        high = dot(operand(base, rows, TALL, (0, 2)), stack(sec, slice(None), slice(256, 512)))
        lane = lax.broadcasted_iota(jnp.int32, (rows, 128), 1)
        logits = jnp.zeros((rows, 128), F32)
        for t, (v, s) in enumerate(((low, 0), (low, 128), (high, 0), (high, 128))):
            v = v[:, s : s + 128]
            sg = sigmoid(v)
            score = jnp.sum(v * sg * head[...], axis=1, keepdims=True)
            push = -sigmoid(-score)
            logits = jnp.where(lane == t, score, logits)
            g = push * head[...] * (sg * (1.0 + v * (1.0 - sg)))
            field[t, pl.ds(base, rows), :] = jnp.where(good, g, 0.0)
        part[pl.ds(base, rows), :] = logits
        return 0

    lax.fori_loop(0, 2, second, 0)
    pick = jnp.where(
        lax.broadcasted_iota(jnp.int32, (16, 128), 0) == lax.broadcasted_iota(jnp.int32, (16, 128), 1), 1.0, 0.0
    ).astype(BF16)
    for x in range(COLS):
        v = dot_t(pick, part[pl.ds((x + 5) * TALL + 5, 128), :].astype(BF16))
        for t in range(4):
            line[t, x : x + 1, :] = v[t : t + 1]
    logit_ref[...] = line[:, :, 0:ROWS].astype(BF16)
    spread(width(5), TALL, 4)

    def second_back(n, _):
        rows = 12 * TALL
        base = pl.multiple_of(n * rows, 16)
        good = valid[pl.ds(base + 6 * (TALL + 1), rows), :] > 0
        v = dot_t(operand(base, rows, TALL, (0, 4)), across(sec))
        g = []
        for t in range(2):
            p = pref[t, pl.ds(base + 2 * (TALL + 1), rows), :]
            g.append(jnp.where(good, v[:, t * 128 : t * 128 + 128] * dsilu(p), 0.0).astype(BF16))
        part[pl.ds(base, rows), :] = dot_t(jnp.concatenate(g, 1), one_w[...])
        return 0

    lax.fori_loop(0, 2, second_back, 0)
    gather_taps(width(3), 3, True, SHORT)

    spread(width(3), SHORT, 1, pix)
    flipped = jnp.concatenate([rgb_taps[8 - n] for n in range(9)], 0)
    back = dot(operand(0, width(2) * SHORT, SHORT, (0, 1)), flipped)
    for t in range(4):
        res[t] = back[:, t * 128 : t * 128 + 128]

    def temper(k, h):
        away = 9 - k - h

        def body(x, _):
            base = pl.multiple_of(x * SHORT, 8)
            good = valid_s[pl.ds((x + 2 - h) * SHORT + 2 - h, SHORT), :] > 0
            for t in range(4):
                p = pre[k, t, pl.ds((x + away) * TALL + away, SHORT), :]
                g = res[t, pl.ds(base, SHORT), :] * dsilu(p)
                field[t, pl.ds(base, SHORT), :] = jnp.where(good, g, 0.0)
            return 0

        lax.fori_loop(0, width(h), body, 0, unroll=2)

    temper(1, 2)

    def back_conv(n, _):
        rows = width(1) * SHORT
        spread(width(2), SHORT, 4)
        k = 1 - n
        near, far = operand(0, rows, SHORT, (0, 2)), operand(0, rows, SHORT, (2, 4))
        high = dot_t(far, across(wide.at[k, 0]))
        low = dot_t(far, across(wide.at[k, 1])) + dot_t(near, across(wide.at[k, 0]))
        for t, (v, s) in enumerate(((low, 0), (low, 128), (high, 0), (high, 128))):
            res[t, 0:rows, :] = v[:, s : s + 128]

        @pl.when(n == 0)
        def _():
            temper(0, 1)

        return 0

    lax.fori_loop(0, 2, back_conv, 0)

    def emit(y, _):
        for t in range(4):
            out_ref[t, y] = res[t, pl.ds(y, COLS, SHORT), :].astype(BF16)
        return 0

    lax.fori_loop(0, ROWS, emit, 0, unroll=4)


def per_device(latent, conv_one, conv_two, to_rgb, disc_one, disc_two, disc_head):
    x = latent[0]

    vmem = pl.BlockSpec(memory_space=pltpu.VMEM)
    hbm = pl.BlockSpec(memory_space=pl.ANY)

    def exchange(first, last, axis):
        n = lax.axis_size(axis)
        before = lax.ppermute(last, axis, [(i, (i + 1) % n) for i in range(n)])
        after = lax.ppermute(first, axis, [((i + 1) % n, i) for i in range(n)])
        return before, after

    first, last = pl.pallas_call(
        cut_columns,
        out_shape=[jax.ShapeDtypeStruct((HALO, 4, ROWS, 128), BF16)] * 2,
        in_specs=[vmem],
        out_specs=[vmem] * 2,
        scratch_shapes=[pltpu.VMEM((4, ROWS * COLS, 128), F32)],
        compiler_params=pltpu.CompilerParams(vmem_limit_bytes=8 << 20),
    )(x)
    left, right = exchange(first, last, "gx")
    first, last = pl.pallas_call(
        cut_rows,
        out_shape=[jax.ShapeDtypeStruct((4, WIDE * HALO, 128), BF16)] * 2,
        in_specs=[vmem] * 3,
        out_specs=[vmem] * 2,
        scratch_shapes=[pltpu.VMEM((2, 4, WIDE * HALO, 128), F32)],
        compiler_params=pltpu.CompilerParams(vmem_limit_bytes=8 << 20),
    )(x, left, right)
    top, bottom = exchange(first, last, "gy")
    taps = lambda k: k.reshape(3, 9, *k.shape[3:])
    rgb_rows = jnp.swapaxes(to_rgb, 3, 4).reshape(81, 128).astype(F32)
    one_rows = jnp.pad(disc_one.reshape(81, 64).astype(F32), ((0, 0), (0, 64)))
    p = WIDE * TALL + PAD
    shapes = [(2, 2, 9, 256, 256), (9, 256, 512), (128, 512), (128, 256), (9, 128, 512), (9, 128, 256)]
    weights = pl.pallas_call(
        lay_out,
        out_shape=[jax.ShapeDtypeStruct(n, BF16) for n in shapes]
        + [jax.ShapeDtypeStruct((WIDE * TALL + PAD, 128), F32)] * 2,
        in_specs=[hbm, hbm, hbm, vmem, vmem],
        out_specs=[vmem] * 8,
        scratch_shapes=[pltpu.VMEM((128, 512), F32), pltpu.SemaphoreType.DMA((24,))],
        compiler_params=pltpu.CompilerParams(vmem_limit_bytes=16 << 20),
        cost_estimate=pl.CostEstimate(flops=0, bytes_accessed=12 << 20, transcendentals=0),
    )(taps(conv_one), taps(conv_two), taps(disc_two), rgb_rows, one_rows)
    out, logits = pl.pallas_call(
        kernel,
        out_shape=[
            jax.ShapeDtypeStruct((4, ROWS, COLS, 128), BF16),
            jax.ShapeDtypeStruct((4, COLS, ROWS), BF16),
        ],
        in_specs=[vmem] * 14,
        out_specs=[vmem, vmem],
        scratch_shapes=[
            pltpu.VMEM((4, p, 128), F32),
            pltpu.VMEM((2, 4, p, 128), F32),
            pltpu.VMEM((4, (COLS + 4) * SHORT, 128), F32),
            pltpu.VMEM((2, p, 128), F32),
            pltpu.VMEM((3, p, 512), BF16),
            pltpu.VMEM((p, 128), F32),
            pltpu.VMEM((p, 128), F32),
            pltpu.VMEM((p, 128), F32),
            pltpu.VMEM((4, COLS, 128), F32),
            pltpu.VMEM((2, 4, WIDE * HALO, 128), F32),
        ],
        compiler_params=pltpu.CompilerParams(vmem_limit_bytes=36 << 20),
    )(x, left, right, top, bottom, *weights, disc_head.reshape(1, 128))
    return out[None], jnp.swapaxes(logits, 1, 2)[None]


def solution(mesh):
    placed = (P(None, None, "gy", "gx", None), P(), P(), P(), P(), P(), P())
    return jax.shard_map(
        per_device,
        mesh=mesh,
        in_specs=placed,
        out_specs=(P(None, None, "gy", "gx", None), P(None, None, "gy", "gx")),
        check_vma=False,
    )
```
